32 devices in a mesh: cuts: 2 (over x), wide: 8 (over z, y), narrow: 2 (over core).
Axes of the slice: x: 2, y: 2, z: 4, core: 2. Of those that a mesh axis runs over, the one named last changes fastest.
Arguments:
- stem_tensor: float32 [2, 16384, 512], P(None, ('cuts', 'wide', 'narrow')), parts along dimension 1, may hold values from -6 to 6
- leaves: bfloat16 [16, 4, 2, 512, 512], P(('cuts', 'wide')), parts along dimension 0, may hold values from -1 to 1
- root_devices: int32 [4], replicated, may hold values from 0 to 7, as said below
- mode_orders: int32 [4, 9], replicated, may hold values from 0 to 8, each once within a row
Outputs:
- contracted: float32 [2, 16384, 512], P(None, ('cuts', 'wide', 'narrow')), parts along dimension 1
The draws below stay inside these ranges and needn't reach their ends.
There are 2 independent parts, one for each index of `cuts`. The reference program is written for one: setup_inputs(seed, part) draws one part's arguments, and reference() takes and returns one part's arrays. A program takes and returns all parts, laid end to end along the dimension named above; an argument that names none is the same for every part. Nothing has to cross between parts.
Inputs may be any that keep to these rules, and one draw needn't show every extreme that they name: `root_devices`: the roots include 0, 4 and 7. `mode_orders`: each row holds every number of 0 to 8 once.
All inputs are finite; a program needn't handle non-finite values.
Results may differ from the reference program's by a relative error of at most 0.0081.
Values may be sent and summed in bfloat16 or wider, within the bound.
No kernel may reach another device: no remote copies, remote signals or barrier semaphores. Data moves between devices by JAX's collectives and lax.ppermute only.
A program may use at most 64 MiB of HBM per device.

```python
import math
import jax
import jax.numpy as jnp
from jax import lax

MODES = 9
BRANCH = 512
ROWS_DEV = 512
STEPS = 4
ROWS = 8192
N_WIDE = 8
N_NARROW = 2


def draw_root_devices(key, part):
    order = jax.random.permutation(jax.random.fold_in(key, 11), STEPS)
    extra = jax.random.randint(jax.random.fold_in(key, 12), (STEPS,), 0, N_WIDE, dtype=jnp.int32)
    position = jnp.arange(STEPS, dtype=jnp.int32)
    fixed_roots = jnp.where(position == 0, 0, jnp.where(position == 1, N_WIDE // 2, N_WIDE - 1)).astype(jnp.int32)
    chosen = jnp.where(position < 3, fixed_roots, extra).astype(jnp.int32)
    return chosen[order].astype(jnp.int32)


def phase_pair(key, count):
    angles = jax.random.uniform(key, (count,), jnp.float32, -math.pi, math.pi)
    return (jnp.cos(angles), jnp.sin(angles))


def unitary_leaf(key):
    count = BRANCH
    index = jnp.arange(count, dtype=jnp.int32)
    table = index[:, None] * index[None, :] % count
    angle = table.astype(jnp.float32) * (2.0 * math.pi / count)
    scale = 1.0 / math.sqrt(count)
    fourier_re = jnp.cos(angle) * scale
    fourier_im = -jnp.sin(angle) * scale
    first_re, first_im = phase_pair(jax.random.fold_in(key, 1), count)
    middle_re, middle_im = phase_pair(jax.random.fold_in(key, 2), count)
    last_re, last_im = phase_pair(jax.random.fold_in(key, 3), count)
    shuffle = jax.random.permutation(jax.random.fold_in(key, 4), count)
    right_re = fourier_re * last_re[None, :] - fourier_im * last_im[None, :]
    right_im = fourier_re * last_im[None, :] + fourier_im * last_re[None, :]
    right_re = right_re[shuffle]
    right_im = right_im[shuffle]
    moved_re = middle_re[:, None] * right_re - middle_im[:, None] * right_im
    moved_im = middle_re[:, None] * right_im + middle_im[:, None] * right_re
    highest = lax.Precision.HIGHEST
    product_re = jnp.dot(fourier_re, moved_re, precision=highest) - jnp.dot(fourier_im, moved_im, precision=highest)
    product_im = jnp.dot(fourier_re, moved_im, precision=highest) + jnp.dot(fourier_im, moved_re, precision=highest)
    final_re = first_re[:, None] * product_re - first_im[:, None] * product_im
    final_im = first_re[:, None] * product_im + first_im[:, None] * product_re
    return jnp.clip(jnp.stack([final_re, final_im]), -1.0, 1.0)


def draw_leaves(key, part):
    keys = jax.random.split(jax.random.fold_in(key, 21), N_WIDE * STEPS)
    matrices = lax.map(unitary_leaf, keys)
    return matrices.reshape(N_WIDE, STEPS, 2, BRANCH, BRANCH).astype(jnp.bfloat16)


def shard_levels(key, dims, cuts, least, top_value):
    def one(dim, parts):
        draws = jax.random.uniform(jax.random.fold_in(jax.random.fold_in(key, 6), dim), (parts,), jnp.float32, least / len(cuts), top_value / len(cuts))
        return jnp.repeat(jnp.exp(draws), dims[dim] // parts).reshape((-1,) + (1,) * (len(dims) - dim - 1))

    loudness = one(*cuts[0])
    for cut in cuts[1:]:
        loudness = loudness * one(*cut)
    return loudness


def scatter_about(own_key, extent, width, most, cuts=(), held_as=jnp.bfloat16):
    array = width * jax.random.normal(own_key, extent, jnp.float32)
    if cuts:
        array = array * shard_levels(own_key, extent, cuts, -0.22, 0.18)
    return jnp.clip(array, -most, most).astype(held_as)


def setup_inputs(seed: int = 0, part: int = 0) -> dict:
    key_of = jax.random.split(jax.random.key(seed), 5)
    own_keys = jax.random.split(jax.random.fold_in(key_of[4], part), 5)
    stem_tensor = scatter_about(own_keys[0], (2, ROWS, BRANCH), 1.0, 6.0, ((1, 16),), jnp.float32)
    leaves = draw_leaves(jax.random.fold_in(jax.random.fold_in(key_of[4], part), 71), part)
    root_devices = draw_root_devices(jax.random.fold_in(key_of[4], 71), part)
    mode_orders = jax.vmap(lambda own: jax.random.permutation(own, MODES))(jax.random.split(key_of[3], STEPS)).reshape((STEPS, MODES)).astype(jnp.int32)
    return {"stem_tensor": stem_tensor, "leaves": leaves, "root_devices": root_devices, "mode_orders": mode_orders}


def complex_product(left_matrix, right_matrix, precision=None):
    real_part = jnp.dot(left_matrix[0], right_matrix[0], preferred_element_type=jnp.float32, precision=precision) - jnp.dot(left_matrix[1], right_matrix[1], preferred_element_type=jnp.float32, precision=precision)
    imag_part = jnp.dot(left_matrix[0], right_matrix[1], preferred_element_type=jnp.float32, precision=precision) + jnp.dot(left_matrix[1], right_matrix[0], preferred_element_type=jnp.float32, precision=precision)
    return jnp.stack([real_part, imag_part])


def column_source(order_row, branch_width):
    column = jnp.arange(branch_width, dtype=jnp.int32)
    mode_count = order_row.shape[0]
    powers = jnp.left_shift(jnp.int32(1), jnp.arange(mode_count, dtype=jnp.int32))
    bit_table = (column[:, None] // powers[None, :]) % 2
    weights = jnp.left_shift(jnp.int32(1), order_row.astype(jnp.int32))
    return jnp.sum(bit_table * weights[None, :], axis=1).astype(jnp.int32)


def reference(stem_tensor, leaves, root_devices, mode_orders):
    network = stem_tensor
    for step_index in range(STEPS):
        group_start = (root_devices[step_index] // 4 * 4).astype(jnp.int32)
        leaf_group = lax.dynamic_slice_in_dim(leaves, group_start, 4, 0)[:, step_index]
        pair_low = complex_product(leaf_group[0], leaf_group[1]).astype(jnp.bfloat16)
        pair_high = complex_product(leaf_group[2], leaf_group[3]).astype(jnp.bfloat16)
        branch = complex_product(pair_low, pair_high)
        ordered = jnp.take(branch, column_source(mode_orders[step_index], BRANCH), axis=2)
        network = complex_product(network, ordered, lax.Precision.HIGHEST)
        if step_index % 2 == 0:
            stem_view = network.reshape(2, N_WIDE, N_NARROW, ROWS_DEV, N_NARROW, BRANCH // N_NARROW)
            network = jnp.swapaxes(stem_view, 2, 4).reshape(network.shape)
    return network
```

```python
import functools

import jax
import jax.numpy as jnp
from jax import lax
from jax.experimental import pallas as pl
from jax.experimental.pallas import tpu as pltpu
from jax.sharding import PartitionSpec as P

F32, BF16, I32 = jnp.float32, jnp.bfloat16, jnp.int32
NN = (((1,), (0,)), ((), ()))
NT = (((1,), (1,)), ((), ()))
CHUNKS = 2
LIMIT = 48 * 1024 * 1024


def dot(left, right, dims=NN):
    return lax.dot_general(left, right, dims, preferred_element_type=F32)


def complex_dot(lr, li, rr, ri, dims=NN):
    return dot(lr, rr, dims) - dot(li, ri, dims), dot(lr, ri, dims) + dot(li, rr, dims)


def source_of(column, modes_ref, step, modes, permuted):
    total = jnp.zeros_like(column)
    for b in range(modes):
        weight = jnp.left_shift(jnp.int32(1), modes_ref[step, b])
        total = total + jnp.where((column >> b) & 1 == 1, weight, 0)
    return jnp.where(permuted == 1, total, column)


def send_kernel(modes, meta_ref, modes_ref, leaf_ref, send_ref):
    rows, width = send_ref.shape[1:]
    y, zb, core = meta_ref[2], meta_ref[3], meta_ref[4]

    @pl.when(y == 0)
    def _():
        send_ref[...] = leaf_ref[:, pl.ds(pl.multiple_of(core * rows, rows), rows), :]

    @pl.when(y == 1)
    def _():
        column = lax.broadcasted_iota(I32, (rows, 1), 0) + core * rows
        source = source_of(column, modes_ref, meta_ref[0], modes, zb)
        picked = lax.broadcasted_iota(I32, (rows, width), 1) == source
        picked = jnp.where(picked, 1.0, 0.0).astype(BF16)
        for p in range(2):
            send_ref[p] = dot(picked, leaf_ref[p], NT).astype(BF16)


def keep_kernel(modes, meta_ref, modes_ref, leaf_ref, keep_ref):
    width = keep_ref.shape[2]
    y, zb = meta_ref[2], meta_ref[3]

    @pl.when(y == 0)
    def _():
        same = lax.broadcasted_iota(I32, (width, width), 0) == lax.broadcasted_iota(
            I32, (width, width), 1
        )
        same = jnp.where(same, 1.0, 0.0).astype(BF16)
        for p in range(2):
            keep_ref[p] = dot(same, leaf_ref[p], NT).astype(BF16)

    @pl.when(y == 1)
    def _():
        column = lax.broadcasted_iota(I32, (1, width), 1)
        source = source_of(column, modes_ref, meta_ref[1], modes, zb)
        picked = lax.broadcasted_iota(I32, (width, width), 0) == source
        picked = jnp.where(picked, 1.0, 0.0).astype(BF16)
        for p in range(2):
            keep_ref[p] = dot(leaf_ref[p], picked).astype(BF16)


def leaf_call(kernel, rows, meta, modes, leaves, which):
    width = leaves.shape[-1]
    return pl.pallas_call(
        functools.partial(kernel, modes.shape[1]),
        grid_spec=pltpu.PrefetchScalarGridSpec(
            num_scalar_prefetch=2,
            grid=(1,),
            in_specs=[
                pl.BlockSpec(
                    (None, None, 2, width, width),
                    lambda i, meta_ref, modes_ref: (0, meta_ref[which], 0, 0, 0),
                )
            ],
            out_specs=pl.BlockSpec((2, rows, width), lambda i, *_: (0, 0, 0)),
        ),
        out_shape=jax.ShapeDtypeStruct((2, rows, width), BF16),
        compiler_params=pltpu.CompilerParams(vmem_limit_bytes=LIMIT),
    )(meta, modes, leaves)


def whole(shape):
    return pl.BlockSpec(shape, lambda i, *_: (0,) * len(shape))


def call(kernel, meta, arrays, outs):
    return pl.pallas_call(
        kernel,
        grid_spec=pltpu.PrefetchScalarGridSpec(
            num_scalar_prefetch=1,
            grid=(1,),
            in_specs=[whole(a.shape) for a in arrays],
            out_specs=[whole(o.shape) for o in outs],
        ),
        out_shape=outs,
        compiler_params=pltpu.CompilerParams(vmem_limit_bytes=LIMIT),
    )(meta, *arrays)


def pair_kernel(meta_ref, left_ref, right_ref, out_ref):
    re, im = complex_dot(left_ref[0], left_ref[1], right_ref[0], right_ref[1])
    out_ref[0] = re.astype(BF16)
    out_ref[1] = im.astype(BF16)


def branch_kernel(chunks, meta_ref, left_ref, *refs):
    own, sib, out_ref = refs[:chunks], refs[chunks : 2 * chunks], refs[-1]
    core = meta_ref[4]
    part = own[0].shape[1]
    half = part * chunks
    re = im = None
    for side, group in ((core, own), (1 - core, sib)):
        for i, ref in enumerate(group):
            at = pl.ds(pl.multiple_of(side * half + i * part, part), part)
            r, m = complex_dot(left_ref[0, :, at], left_ref[1, :, at], ref[0], ref[1])
            re, im = (r, m) if re is None else (re + r, im + m)
    out_ref[0] = re.astype(BF16)
    out_ref[1] = im.astype(BF16)


def pick(first, one_ref, other_ref):
    return [jnp.where(first, one_ref[p], other_ref[p]) for p in range(2)]


def early_kernel(chunks, meta_ref, own_ref, sib_ref, *refs):
    mine, cross, mine_sib, cross_sib = (refs[i * chunks : (i + 1) * chunks] for i in range(4))
    own_out, sib_out = refs[4 * chunks :]
    first = meta_ref[2] == 0
    stems = [[ref[p].astype(BF16) for p in range(2)] for ref in (own_ref, sib_ref)]
    second = []
    for near, far in ((mine, cross), (mine_sib, cross_sib)):
        parts = [pick(first, b, a) for a, b in zip(near, far)]
        second.append([jnp.concatenate([q[p] for q in parts], 0) for p in range(2)])
    for near, far, out_ref in ((mine, cross, own_out), (mine_sib, cross_sib, sib_out)):
        parts = [pick(first, a, b) for a, b in zip(near, far)]
        turned = [jnp.concatenate([q[p] for q in parts], 0) for p in range(2)]
        re = im = None
        for stem, right in zip(stems, second):
            r, m = complex_dot(*stem, *turned, NT)
            r, m = complex_dot(r.astype(BF16), m.astype(BF16), *right)
            re, im = (r, m) if re is None else (re + r, im + m)
        out_ref[0] = re.astype(BF16)
        out_ref[1] = im.astype(BF16)


def late_kernel(chunks, meta_ref, own_ref, sib_ref, *refs):
    mine, cross, mine_sib, cross_sib = (refs[i * chunks : (i + 1) * chunks] for i in range(4))
    out_ref = refs[-1]
    first = meta_ref[2] == 0
    parts = [pick(first, a, b) for a, b in zip(mine, cross)]
    turned = [jnp.concatenate([q[p] for q in parts], 0) for p in range(2)]
    re = im = None
    for net, near, far in ((own_ref, mine, cross), (sib_ref, mine_sib, cross_sib)):
        parts = [pick(first, b, a) for a, b in zip(near, far)]
        right = [jnp.concatenate([q[p] for q in parts], 0) for p in range(2)]
        r, m = complex_dot(net[0], net[1], *turned, NT)
        r, m = complex_dot(r.astype(BF16), m.astype(BF16), *right)
        re, im = (r, m) if re is None else (re + r, im + m)
    out_ref[0] = re
    out_ref[1] = im


def swap(value, axis, bit, among=lambda i: True):
    n = lax.axis_size(axis)
    return lax.ppermute(value, axis, [(i, i ^ bit) for i in range(n) if among(i)])


def holds(i):
    return i >> 1 & 1 == i & 1


def after(value, *others):
    return lax.optimization_barrier((value, *others))[0]


def local(stem_tensor, leaves, root_devices, mode_orders):
    steps, width = leaves.shape[1], stem_tensor.shape[2]
    wide = lax.axis_size("wide")
    half = width // lax.axis_size("narrow")
    part = half // CHUNKS
    w = lax.axis_index("wide")
    core = lax.axis_index("narrow")
    y, zb, group = w & 1, w >> 1 & 1, w >> 2
    holder = y == zb
    piece = jax.ShapeDtypeStruct((2, part, width), BF16)

    own_stem = stem_tensor.astype(BF16)
    sib_stem = swap(own_stem, "narrow", 1)

    branches = []
    gate = ()
    for j in range(steps // 2):
        k_keep = 2 * j + y
        k_send = 2 * j + 1 - y
        meta = jnp.stack([k_send, k_keep, y, zb, core]).astype(I32)
        send = leaf_call(send_kernel, half, meta, mode_orders, leaves, 0)
        keep = leaf_call(keep_kernel, width, meta, mode_orders, leaves, 1)
        pairs = []
        got = []
        for i in range(CHUNKS):
            chunk = send[:, i * part : (i + 1) * part]
            if gate:
                chunk = after(chunk, gate[i])
            left = swap(chunk, "wide", 1)
            got.append(left)
            pairs.append(call(pair_kernel, meta, [left, keep], [piece])[0])
        gate = got
        sibs = [swap(p, "narrow", 1) for p in pairs]
        out = []
        for i in range(CHUNKS):
            low = swap(pairs[i], "wide", 2, lambda i: not holds(i))
            [made] = call(
                functools.partial(branch_kernel, CHUNKS), meta, [low, *pairs, *sibs], [piece]
            )
            out.append(made)
        owner = root_devices[k_keep] // 4
        mine = []
        cross = []
        for made in out:
            if wide == 8:
                other = swap(made, "wide", 4, holds)
                made = jnp.where(owner == group, made, other)
                passed = swap(made, "wide", 2, holds)
                made = jnp.where(holder, made, passed)
                mine.append(made)
                cross.append(swap(made, "wide", 1))
            else:
                good = holder & (owner == group)
                both = [
                    lax.psum(jnp.where(good & (y == side), made, jnp.zeros_like(made)), "wide")
                    for side in range(2)
                ]
                mine.append(jnp.where(y == 0, both[0], both[1]))
                cross.append(jnp.where(y == 0, both[1], both[0]))
        branches.append(
            [
                *mine,
                *cross,
                *[swap(m, "narrow", 1) for m in mine],
                *[swap(m, "narrow", 1) for m in cross],
            ]
        )

    middle = jax.ShapeDtypeStruct((2, stem_tensor.shape[1], width), BF16)
    own, sib = call(
        functools.partial(early_kernel, CHUNKS),
        meta,
        [own_stem, sib_stem, *branches[0]],
        [middle, middle],
    )
    result = jax.ShapeDtypeStruct(stem_tensor.shape, F32)
    return call(functools.partial(late_kernel, CHUNKS), meta, [own, sib, *branches[1]], [result])[0]


def solution(mesh):
    placed = (
        P(None, ("cuts", "wide", "narrow"), None),
        P(("cuts", "wide"), None, None, None, None),
        P(),
        P(),
    )
    return jax.shard_map(
        local,
        mesh=mesh,
        in_specs=placed,
        out_specs=P(None, ("cuts", "wide", "narrow"), None),
        check_vma=False,
    )
```

```python
import functools

import jax
import jax.numpy as jnp
from jax import lax
from jax.experimental import pallas as pl
from jax.experimental.pallas import tpu as pltpu
from jax.sharding import PartitionSpec as P

F32, BF16, I32 = jnp.float32, jnp.bfloat16, jnp.int32
NN = (((1,), (0,)), ((), ()))
NT = (((1,), (1,)), ((), ()))
LIMIT = 48 * 1024 * 1024


def dot(left, right, dims=NN):
    return lax.dot_general(left, right, dims, preferred_element_type=F32)


def complex_dot(lr, li, rr, ri, dims=NN):
    return dot(lr, rr, dims) - dot(li, ri, dims), dot(lr, ri, dims) + dot(li, rr, dims)


def source_of(column, modes_ref, step, modes, permuted):
    total = jnp.zeros_like(column)
    for b in range(modes):
        weight = jnp.left_shift(jnp.int32(1), modes_ref[step, b])
        total = total + jnp.where((column >> b) & 1 == 1, weight, 0)
    return jnp.where(permuted == 1, total, column)


def send_kernel(modes, meta_ref, modes_ref, leaf_ref, send_ref):
    rows, width = send_ref.shape[1:]
    y, zb, core = meta_ref[2], meta_ref[3], meta_ref[4]

    @pl.when(y == 0)
    def _():
        send_ref[...] = leaf_ref[:, pl.ds(pl.multiple_of(core * rows, rows), rows), :]

    @pl.when(y == 1)
    def _():
        column = lax.broadcasted_iota(I32, (rows, 1), 0) + core * rows
        source = source_of(column, modes_ref, meta_ref[0], modes, zb)
        picked = lax.broadcasted_iota(I32, (rows, width), 1) == source
        picked = jnp.where(picked, 1.0, 0.0).astype(BF16)
        for p in range(2):
            send_ref[p] = dot(picked, leaf_ref[p], NT).astype(BF16)


def keep_kernel(modes, meta_ref, modes_ref, leaf_ref, keep_ref):
    width = keep_ref.shape[2]
    y, zb = meta_ref[2], meta_ref[3]

    @pl.when(y == 0)
    def _():
        same = lax.broadcasted_iota(I32, (width, width), 0) == lax.broadcasted_iota(
            I32, (width, width), 1
        )
        same = jnp.where(same, 1.0, 0.0).astype(BF16)
        for p in range(2):
            keep_ref[p] = dot(same, leaf_ref[p], NT).astype(BF16)

    @pl.when(y == 1)
    def _():
        column = lax.broadcasted_iota(I32, (1, width), 1)
        source = source_of(column, modes_ref, meta_ref[1], modes, zb)
        picked = lax.broadcasted_iota(I32, (width, width), 0) == source
        picked = jnp.where(picked, 1.0, 0.0).astype(BF16)
        for p in range(2):
            keep_ref[p] = dot(leaf_ref[p], picked).astype(BF16)


def leaf_call(kernel, rows, meta, modes, leaves, which):
    width = leaves.shape[-1]
    return pl.pallas_call(
        functools.partial(kernel, modes.shape[1]),
        grid_spec=pltpu.PrefetchScalarGridSpec(
            num_scalar_prefetch=2,
            grid=(1,),
            in_specs=[
                pl.BlockSpec(
                    (None, None, 2, width, width),
                    lambda i, meta_ref, modes_ref: (0, meta_ref[which], 0, 0, 0),
                )
            ],
            out_specs=pl.BlockSpec((2, rows, width), lambda i, *_: (0, 0, 0)),
        ),
        out_shape=jax.ShapeDtypeStruct((2, rows, width), BF16),
        compiler_params=pltpu.CompilerParams(vmem_limit_bytes=LIMIT),
    )(meta, modes, leaves)


def whole(shape):
    return pl.BlockSpec(shape, lambda i, *_: (0,) * len(shape))


def call(kernel, meta, arrays, outs):
    return pl.pallas_call(
        kernel,
        grid_spec=pltpu.PrefetchScalarGridSpec(
            num_scalar_prefetch=1,
            grid=(1,),
            in_specs=[whole(a.shape) for a in arrays],
            out_specs=[whole(o.shape) for o in outs],
        ),
        out_shape=outs,
        compiler_params=pltpu.CompilerParams(vmem_limit_bytes=LIMIT),
    )(meta, *arrays)


def pair_kernel(meta_ref, left_ref, right_ref, out_ref):
    re, im = complex_dot(left_ref[0], left_ref[1], right_ref[0], right_ref[1])
    out_ref[0] = re.astype(BF16)
    out_ref[1] = im.astype(BF16)


def branch_kernel(meta_ref, own_ref, got_ref, own_sib_ref, got_sib_ref, first_ref, second_ref):
    y, zb, core = meta_ref[2], meta_ref[3], meta_ref[4]
    rows, width = own_ref.shape[1:]
    part = rows // 2
    high_here = y == zb

    def multiply(left_ref, near_ref, far_ref):
        re = im = None
        for side, ref in ((core, near_ref), (1 - core, far_ref)):
            at = pl.ds(pl.multiple_of(side * rows, rows), rows)
            r, m = complex_dot(left_ref[0, :, at], left_ref[1, :, at], ref[0], ref[1])
            re, im = (r, m) if re is None else (re + r, im + m)
        return re.astype(BF16), im.astype(BF16)

    def store(p, top, bottom):
        @pl.when(zb == 0)
        def _():
            first_ref[p] = top
            second_ref[p] = bottom

        @pl.when(zb == 1)
        def _():
            first_ref[p] = bottom
            second_ref[p] = top

    def finish(parts):
        @pl.when(y == 1)
        def _():
            for p, value in enumerate(parts):
                store(p, value[:part], value[part:])

        @pl.when(y == 0)
        def _():
            same = lax.broadcasted_iota(I32, (width, width), 0) == lax.broadcasted_iota(
                I32, (width, width), 1
            )
            same = jnp.where(same, 1.0, 0.0).astype(BF16)
            for p, value in enumerate(parts):
                turned = dot(same, value, NT).astype(BF16)
                both = jnp.concatenate([turned[:rows], turned[rows:]], 1)
                store(p, both[:part], both[part:])

    @pl.when(high_here)
    def _():
        finish(multiply(got_ref, own_ref, own_sib_ref))

    @pl.when(jnp.logical_not(high_here))
    def _():
        finish(multiply(own_ref, got_ref, got_sib_ref))


def stem_kernel(meta_ref, own_ref, sib_ref, *refs):
    pieces, (out_ref, o_ref, n1_ref, sem) = refs[:-4], refs[-4:]
    items = len(pieces) // 4
    zb, core, y = meta_ref[0], meta_ref[1], meta_ref[2]
    part, width = pieces[0].shape[1:]
    half = width // 2
    copies = []
    for m in range(items):
        step = meta_ref[3 + m]
        column = y if m % 2 == 0 else 1 - y
        for q in range(4):
            side = core if q < 2 else 1 - core
            h = zb if q % 2 == 0 else 1 - zb
            for s in range(2):
                row = jnp.where(column == 1, side, s) * half + h * part
                col = jnp.where(column == 1, s, side) * half
                copy = pltpu.make_async_copy(
                    pieces[4 * m + q].at[:, :, s * half : (s + 1) * half],
                    o_ref.at[
                        step,
                        :,
                        pl.ds(pl.multiple_of(row, part), part),
                        pl.ds(pl.multiple_of(col, half), half),
                    ],
                    sem.at[8 * m + 2 * q + s],
                )
                copy.start()
                copies.append(copy)
    for copy in copies:
        copy.wait()
    for f, ref in ((core, own_ref), (1 - core, sib_ref)):
        at = pl.ds(pl.multiple_of(f * half, half), half)
        t = complex_dot(ref[0], ref[1], o_ref[0, 0], o_ref[0, 1])
        for p in range(2):
            value = t[p].astype(BF16)
            for e in range(2):
                n1_ref[e, p, :, at] = value[:, e * half : (e + 1) * half]
    mine = pl.ds(pl.multiple_of(core * half, half), half)
    o12 = complex_dot(o_ref[1, 0], o_ref[1, 1], o_ref[2, 0, :, mine], o_ref[2, 1, :, mine])
    o12 = [v.astype(BF16) for v in o12]
    re = im = None
    for e in range(2):
        at = slice(e * half, (e + 1) * half)
        n4 = complex_dot(n1_ref[e, 0], n1_ref[e, 1], *o12)
        r, m = complex_dot(
            n4[0].astype(BF16), n4[1].astype(BF16), o_ref[3, 0, at, :], o_ref[3, 1, at, :]
        )
        re, im = (r, m) if re is None else (re + r, im + m)
    out_ref[0] = re
    out_ref[1] = im


def stem_call(meta, own, sib, items):
    shape = own.shape
    width = shape[2]
    pieces = [piece for item in items for piece in item]
    return pl.pallas_call(
        stem_kernel,
        grid_spec=pltpu.PrefetchScalarGridSpec(
            num_scalar_prefetch=1,
            grid=(1,),
            in_specs=[whole(shape)] * 2 + [pl.BlockSpec(memory_space=pl.ANY)] * len(pieces),
            out_specs=whole(shape),
            scratch_shapes=[
                pltpu.VMEM((len(items), 2, width, width), BF16),
                pltpu.VMEM((2, *shape), BF16),
                pltpu.SemaphoreType.DMA((2 * len(pieces),)),
            ],
        ),
        out_shape=jax.ShapeDtypeStruct(shape, F32),
        compiler_params=pltpu.CompilerParams(vmem_limit_bytes=LIMIT),
    )(meta, own, sib, *pieces)


def swap(value, axis, bit):
    n = lax.axis_size(axis)
    return lax.ppermute(value, axis, [(i, i ^ bit) for i in range(n)])


def other_core(value):
    return swap(value, "narrow", 1)


def tree(leaves, modes, k_keep, k_send, y, zb, core):
    width = leaves.shape[-1]
    rows = width // lax.axis_size("narrow")
    meta = jnp.stack([k_send, k_keep, y, zb, core]).astype(I32)
    send = leaf_call(send_kernel, rows, meta, modes, leaves, 0)
    keep = leaf_call(keep_kernel, width, meta, modes, leaves, 1)
    left = swap(send, "wide", 1)
    [pair] = call(pair_kernel, meta, [left, keep], [jax.ShapeDtypeStruct(left.shape, BF16)])
    got = swap(pair, "wide", 2)
    piece = jax.ShapeDtypeStruct((2, rows // 2, width), BF16)
    return call(
        branch_kernel, meta, [pair, got, other_core(pair), other_core(got)], [piece, piece]
    )


def item_of(first, second):
    return [first, second, other_core(first), other_core(second)]


def each_own_two(own_stem, sib_stem, leaves, owners, modes, y, zb, group, core):
    def steps_of(g):
        index = jnp.arange(owners.shape[0], dtype=I32)
        mine = owners == g
        low = jnp.min(jnp.where(mine, index, owners.shape[0] - 1))
        high = jnp.max(jnp.where(mine, index, 0))
        return jnp.where(y == 0, low, high), jnp.where(y == 0, high, low)

    keep, send = steps_of(group)
    far_keep, far_send = steps_of(1 - group)
    first, second = tree(leaves, modes, keep, send, y, zb, core)
    far = swap(first, "wide", 4)
    near = [item_of(first, second), item_of(swap(first, "wide", 1), swap(second, "wide", 1))]
    far_second = swap(far, "wide", 2)
    away = [item_of(far, far_second), item_of(swap(far, "wide", 1), swap(far_second, "wide", 1))]
    meta = jnp.stack([zb, core, y, keep, send, far_keep, far_send]).astype(I32)
    return stem_call(meta, own_stem, sib_stem, near + away)


def any_owners(own_stem, sib_stem, leaves, owners, modes, y, zb, group, core):
    items, order = [], []
    two = lax.axis_size("wide") == 8
    for j in range(leaves.shape[1] // 2):
        keep, send = 2 * j + y, 2 * j + 1 - y
        first, second = tree(leaves, modes, keep, send, y, zb, core)
        owned = owners[keep] == group
        if two:
            first = jnp.where(owned, first, swap(first, "wide", 4))
            second = swap(first, "wide", 2)
            cross = [swap(first, "wide", 1), swap(second, "wide", 1)]
        else:
            sums = [
                lax.psum(
                    jnp.where(owned & (zb == 0) & (y == side), v, jnp.zeros_like(v)), "wide"
                )
                for side in range(2)
                for v in (first, second)
            ]
            first, second = (jnp.where(y == 0, a, b) for a, b in zip(sums[:2], sums[2:]))
            cross = [jnp.where(y == 0, b, a) for a, b in zip(sums[:2], sums[2:])]
        items += [item_of(first, second), item_of(*cross)]
        order += [keep, send]
    meta = jnp.stack([zb if two else jnp.zeros_like(zb), core, y, *order]).astype(I32)
    return stem_call(meta, own_stem, sib_stem, items)


MODE = "cond"


def local(stem_tensor, leaves, root_devices, mode_orders):
    w = lax.axis_index("wide")
    core = lax.axis_index("narrow")
    y, zb, group = w & 1, w >> 1 & 1, w >> 2
    owners = root_devices // 4
    own_stem = stem_tensor.astype(BF16)
    given = (own_stem, other_core(own_stem), leaves, owners, mode_orders, y, zb, group, core)
    if lax.axis_size("wide") != 8 or MODE == "four":
        return any_owners(*given)
    if MODE == "two":
        return each_own_two(*given)
    return lax.cond(jnp.sum(owners) == 2, each_own_two, any_owners, *given)


def solution(mesh):
    placed = (
        P(None, ("cuts", "wide", "narrow"), None),
        P(("cuts", "wide"), None, None, None, None),
        P(),
        P(),
    )
    return jax.shard_map(
        local,
        mesh=mesh,
        in_specs=placed,
        out_specs=P(None, ("cuts", "wide", "narrow"), None),
        check_vma=False,
    )
```

```python
import functools

import jax
import jax.numpy as jnp
from jax import lax
from jax.experimental import pallas as pl
from jax.experimental.pallas import tpu as pltpu
from jax.sharding import PartitionSpec as P

F32, BF16, I32 = jnp.float32, jnp.bfloat16, jnp.int32
NN = (((1,), (0,)), ((), ()))
NT = (((1,), (1,)), ((), ()))
LIMIT = 48 * 1024 * 1024
LEAF_LIMIT = 61 * 1024 * 1024
CHUNKS_TWO, CHUNKS_FOUR = 2, 1


def dot(left, right, dims=NN):
    return lax.dot_general(left, right, dims, preferred_element_type=F32)


def complex_dot(lr, li, rr, ri, dims=NN):
    return dot(lr, rr, dims) - dot(li, ri, dims), dot(lr, ri, dims) + dot(li, rr, dims)


def source_of(column, modes_ref, step, modes, permuted):
    total = jnp.zeros_like(column)
    for b in range(modes):
        weight = jnp.left_shift(jnp.int32(1), modes_ref[step, b])
        total = total + jnp.where((column >> b) & 1 == 1, weight, 0)
    return jnp.where(permuted == 1, total, column)


def place():
    w = lax.axis_index("wide")
    return w & 1, w >> 1 & 1, w >> 2, lax.axis_index("narrow")


def steps_of(plan, roots_ref, y, group):
    if plan is not None:
        low, high = (jnp.int32(k) for k in plan)
    else:
        low = high = None
        for k in range(roots_ref.shape[0]):
            mine = roots_ref[k] >> 2 == group
            high = jnp.where(mine, k, 0 if high is None else high)
        for k in reversed(range(roots_ref.shape[0])):
            mine = roots_ref[k] >> 2 == group
            low = jnp.where(mine, k, k if low is None else low)
    return jnp.where(y == 0, low, high), jnp.where(y == 0, high, low)


def send_kernel(plan, roots_ref, modes_ref, leaves_ref, *refs):
    sends, (leaf_ref, sem) = refs[:-2], refs[-2:]
    part, width = sends[0].shape[1:]
    rows = part * len(sends)
    y, zb, group, core = place()
    _, step = steps_of(plan, roots_ref, y, group)

    @pl.when(y == 0)
    def _():
        copies = []
        for i, send_ref in enumerate(sends):
            at = pl.ds(pl.multiple_of(core * rows + i * part, part), part)
            copies.append(
                pltpu.make_async_copy(leaves_ref.at[0, step, :, at], send_ref, sem.at[i])
            )
            copies[-1].start()
        for copy in copies:
            copy.wait()

    @pl.when(y == 1)
    def _():
        copy = pltpu.make_async_copy(leaves_ref.at[0, step], leaf_ref, sem.at[0])
        copy.start()
        column = lax.broadcasted_iota(I32, (rows, 1), 0) + core * rows
        source = source_of(column, modes_ref, step, modes_ref.shape[1], zb)
        picked = lax.broadcasted_iota(I32, (rows, width), 1) == source
        picked = jnp.where(picked, 1.0, 0.0).astype(BF16)
        copy.wait()
        for p in range(2):
            made = dot(picked, leaf_ref[p], NT).astype(BF16)
            for i, send_ref in enumerate(sends):
                send_ref[p] = made[i * part : (i + 1) * part]


def keep_kernel(plan, roots_ref, modes_ref, leaves_ref, keep_ref, leaf_ref, sem):
    width = keep_ref.shape[2]
    y, zb, group, core = place()
    step, _ = steps_of(plan, roots_ref, y, group)
    copy = pltpu.make_async_copy(leaves_ref.at[0, step], leaf_ref, sem.at[0])
    copy.start()
    copy.wait()

    @pl.when(y == 0)
    def _():
        same = lax.broadcasted_iota(I32, (width, width), 0) == lax.broadcasted_iota(
            I32, (width, width), 1
        )
        same = jnp.where(same, 1.0, 0.0).astype(BF16)
        for p in range(2):
            keep_ref[p] = dot(same, leaf_ref[p], NT).astype(BF16)

    @pl.when(y == 1)
    def _():
        column = lax.broadcasted_iota(I32, (1, width), 1)
        source = source_of(column, modes_ref, step, modes_ref.shape[1], zb)
        picked = lax.broadcasted_iota(I32, (width, width), 0) == source
        picked = jnp.where(picked, 1.0, 0.0).astype(BF16)
        for p in range(2):
            keep_ref[p] = dot(leaf_ref[p], picked).astype(BF16)


def leaf_call(kernel, parts, rows, plan, roots, modes, leaves):
    width = leaves.shape[-1]
    return pl.pallas_call(
        functools.partial(kernel, plan),
        grid_spec=pltpu.PrefetchScalarGridSpec(
            num_scalar_prefetch=2,
            grid=(1,),
            in_specs=[pl.BlockSpec(memory_space=pl.ANY)],
            out_specs=[whole((2, rows, width))] * parts,
            scratch_shapes=[pltpu.VMEM((2, width, width), BF16), pltpu.SemaphoreType.DMA((parts,))],
        ),
        out_shape=[jax.ShapeDtypeStruct((2, rows, width), BF16)] * parts,
        compiler_params=pltpu.CompilerParams(vmem_limit_bytes=LEAF_LIMIT),
    )(roots, modes, leaves)


def whole(shape):
    return pl.BlockSpec(shape, lambda i, *_: (0,) * len(shape))


def call(kernel, arrays, outs):
    return pl.pallas_call(
        kernel,
        grid=(1,),
        in_specs=[whole(a.shape) for a in arrays],
        out_specs=[whole(o.shape) for o in outs],
        out_shape=outs,
        compiler_params=pltpu.CompilerParams(vmem_limit_bytes=LIMIT),
    )(*arrays)


def pair_kernel(left_ref, right_ref, out_ref):
    re, im = complex_dot(left_ref[0], left_ref[1], right_ref[0], right_ref[1])
    out_ref[0] = re.astype(BF16)
    out_ref[1] = im.astype(BF16)


def branch_kernel(chunks, *refs):
    own, got, own_sib, got_sib = (refs[i * chunks : (i + 1) * chunks] for i in range(4))
    first_ref, second_ref = refs[4 * chunks : 4 * chunks + 2]
    both_ref = refs[4 * chunks + 2] if len(refs) > 4 * chunks + 2 else None
    y, zb, _, core = place()
    rows, width = own[0].shape[1] * chunks, own[0].shape[2]
    part = rows // 2
    high_here = y == zb

    def joined(group, p, at=slice(None)):
        values = [ref[p, :, at] for ref in group]
        return values[0] if len(values) == 1 else jnp.concatenate(values, 0)

    def multiply(left, near, far):
        re = im = None
        for side, right in ((core, near), (1 - core, far)):
            at = pl.ds(pl.multiple_of(side * rows, rows), rows)
            r, m = complex_dot(
                joined(left, 0, at), joined(left, 1, at), joined(right, 0), joined(right, 1)
            )
            re, im = (r, m) if re is None else (re + r, im + m)
        return re.astype(BF16), im.astype(BF16)

    def store(p, top, bottom):
        @pl.when(zb == 0)
        def _():
            first_ref[p] = top
            second_ref[p] = bottom
            if both_ref is not None:
                both_ref[0, p] = top
                both_ref[1, p] = bottom

        @pl.when(zb == 1)
        def _():
            first_ref[p] = bottom
            second_ref[p] = top
            if both_ref is not None:
                both_ref[0, p] = bottom
                both_ref[1, p] = top

    def finish(parts):
        @pl.when(y == 1)
        def _():
            for p, value in enumerate(parts):
                store(p, value[:part], value[part:])

        @pl.when(y == 0)
        def _():
            same = lax.broadcasted_iota(I32, (rows, rows), 0) == lax.broadcasted_iota(
                I32, (rows, rows), 1
            )
            same = jnp.where(same, 1.0, 0.0).astype(BF16)
            for p, value in enumerate(parts):
                turned = [dot(same, value[:, i : i + rows], NT) for i in range(0, width, rows)]
                both = jnp.concatenate(turned, 1).astype(BF16)
                store(p, both[:part], both[part:])

    @pl.when(high_here)
    def _():
        finish(multiply(got, own, own_sib))

    @pl.when(jnp.logical_not(high_here))
    def _():
        finish(multiply(own, got, got_sib))


def halves(ref, count):
    return [ref] if count == 1 else [ref.at[h] for h in range(count)]


def stem_kernel(plans, turn, layout, roots_ref, own_hbm, sib_hbm, *refs):
    pieces, (out_hbm, o_ref, n1_ref, own_ref, sib_ref, out_ref, sem) = refs[:-7], refs[-7:]
    pieces = [piece for ref, n in zip(pieces, layout) for piece in halves(ref, n)]
    items = len(pieces) // 4
    y, zb, group, core = place()
    zb = zb if turn else 0
    part, width = pieces[0].shape[1:]
    half = width // 2
    first = [
        pltpu.make_async_copy(own_hbm, own_ref, sem.at[items]),
        pltpu.make_async_copy(sib_hbm, sib_ref, sem.at[items + 1]),
    ]
    for copy in first:
        copy.start()
    for m in range(items):
        plan = plans[m // 2] if plans else None
        steps = steps_of(plan, roots_ref, y, group if m < 2 else 1 - group)
        step = steps[m % 2]
        column = y if m % 2 == 0 else 1 - y
        for q in range(4):
            side = core if q < 2 else 1 - core
            h = zb if q % 2 == 0 else 1 - zb
            for s in range(2):
                row = jnp.where(column == 1, side, s) * half + h * part
                col = jnp.where(column == 1, s, side) * half
                pltpu.make_async_copy(
                    pieces[4 * m + q].at[:, :, s * half : (s + 1) * half],
                    o_ref.at[
                        step,
                        :,
                        pl.ds(pl.multiple_of(row, part), part),
                        pl.ds(pl.multiple_of(col, half), half),
                    ],
                    sem.at[step],
                ).start()

    def arrived(step):
        pltpu.make_async_copy(o_ref.at[step], o_ref.at[step], sem.at[step]).wait()

    for copy in first:
        copy.wait()
    arrived(0)
    for f, ref in ((core, own_ref), (1 - core, sib_ref)):
        at = pl.ds(pl.multiple_of(f * half, half), half)
        t = complex_dot(ref[0], ref[1], o_ref[0, 0], o_ref[0, 1])
        for p in range(2):
            value = t[p].astype(BF16)
            for e in range(2):
                n1_ref[e, p, :, at] = value[:, e * half : (e + 1) * half]
    mine = pl.ds(pl.multiple_of(core * half, half), half)
    arrived(1)
    arrived(2)
    o12 = complex_dot(o_ref[1, 0], o_ref[1, 1], o_ref[2, 0, :, mine], o_ref[2, 1, :, mine])
    o12 = [v.astype(BF16) for v in o12]
    arrived(3)
    rows = own_ref.shape[1]
    copies = []
    for r in range(2):
        band = slice(r * rows // 2, (r + 1) * rows // 2)
        n4 = [complex_dot(n1_ref[e, 0, band], n1_ref[e, 1, band], *o12) for e in range(2)]
        n4 = [jnp.concatenate([n4[0][p], n4[1][p]], 1).astype(BF16) for p in range(2)]
        made = complex_dot(*n4, o_ref[3, 0], o_ref[3, 1])
        for p in range(2):
            out_ref[p, band] = made[p]
        copy = pltpu.make_async_copy(
            out_ref.at[:, band], out_hbm.at[:, band], sem.at[items + 2 + r]
        )
        copy.start()
        copies.append(copy)
    for copy in copies:
        copy.wait()


def stem_call(plans, turn, roots, own, sib, items):
    shape = own.shape
    width = shape[2]
    pieces = [piece for item in items for piece in item]
    layout = tuple(piece.ndim == 4 and piece.shape[0] or 1 for piece in pieces)
    anywhere = pl.BlockSpec(memory_space=pl.ANY)
    return pl.pallas_call(
        functools.partial(stem_kernel, plans, turn, layout),
        grid_spec=pltpu.PrefetchScalarGridSpec(
            num_scalar_prefetch=1,
            grid=(1,),
            in_specs=[anywhere] * (2 + len(pieces)),
            out_specs=anywhere,
            scratch_shapes=[
                pltpu.VMEM((len(items), 2, width, width), BF16),
                pltpu.VMEM((2, *shape), BF16),
                pltpu.VMEM(shape, BF16),
                pltpu.VMEM(shape, BF16),
                pltpu.VMEM(shape, F32),
                pltpu.SemaphoreType.DMA((len(items) + 4,)),
            ],
        ),
        out_shape=jax.ShapeDtypeStruct(shape, F32),
        compiler_params=pltpu.CompilerParams(vmem_limit_bytes=LIMIT),
    )(roots, own, sib, *pieces)


def swap(value, axis, bit):
    n = lax.axis_size(axis)
    return lax.ppermute(value, axis, [(i, i ^ bit) for i in range(n)])


def other_core(value):
    return swap(value, "narrow", 1)


def tree(leaves, roots, modes, plan, chunks, joint):
    width = leaves.shape[-1]
    rows = width // lax.axis_size("narrow")
    sends = leaf_call(send_kernel, chunks, rows // chunks, plan, roots, modes, leaves)
    [keep] = leaf_call(keep_kernel, 1, width, plan, roots, modes, leaves)
    lefts = [swap(send, "wide", 1) for send in sends]
    pairs = [
        call(pair_kernel, [left, keep], [jax.ShapeDtypeStruct(left.shape, BF16)])[0]
        for left in lefts
    ]
    gots = [swap(pair, "wide", 2) for pair in pairs]
    sibs = [other_core(v) for v in pairs + gots]
    piece = jax.ShapeDtypeStruct((2, rows // 2, width), BF16)
    outs = [piece, piece]
    if joint:
        outs.append(jax.ShapeDtypeStruct((2, *piece.shape), BF16))
    return call(functools.partial(branch_kernel, chunks), pairs + gots + sibs, outs)


def item_of(first, second):
    return [first, second, other_core(first), other_core(second)]


def each_own_two(stem, leaves, roots, modes):
    own = stem.astype(BF16)
    sib = other_core(own)
    first, _, both = tree(leaves, roots, modes, None, CHUNKS_TWO, True)
    far = swap(first, "wide", 4)
    cross = swap(both, "wide", 1)
    near = [[both, other_core(both)], [cross, other_core(cross)]]
    far_second = swap(far, "wide", 2)
    away = [item_of(far, far_second), item_of(swap(far, "wide", 1), swap(far_second, "wide", 1))]
    return stem_call(None, True, roots, own, sib, near + away)


def any_owners(stem, leaves, roots, modes):
    y, zb, group, _ = place()
    own = stem.astype(BF16)
    sib = other_core(own)
    two = lax.axis_size("wide") == 8
    items, plans = [], []
    for j in range(leaves.shape[1] // 2):
        plan = (2 * j, 2 * j + 1)
        first, second = tree(leaves, roots, modes, plan, CHUNKS_FOUR, False)
        owned = roots[2 * j + y] // 4 == group
        if two:
            here = jnp.where(owned, first, swap(first, "wide", 4))
            second = swap(here, "wide", 2)
            cross = [swap(here, "wide", 1), swap(second, "wide", 1)]
        else:
            sums = [
                lax.psum(
                    jnp.where(owned & (zb == 0) & (y == side), v, jnp.zeros_like(v)), "wide"
                )
                for side in range(2)
                for v in (first, second)
            ]
            here, second = (jnp.where(y == 0, a, b) for a, b in zip(sums[:2], sums[2:]))
            cross = [jnp.where(y == 0, b, a) for a, b in zip(sums[:2], sums[2:])]
        items += [item_of(here, second), item_of(*cross)]
        plans.append(plan)
    return stem_call(tuple(plans), two, roots, own, sib, items)


MODE = "cond"


def local(stem_tensor, leaves, root_devices, mode_orders):
    given = (stem_tensor, leaves, root_devices, mode_orders)
    if lax.axis_size("wide") != 8 or MODE == "four":
        return any_owners(*given)
    if MODE == "two":
        return each_own_two(*given)
    return lax.cond(jnp.sum(root_devices // 4) == 2, each_own_two, any_owners, *given)


def solution(mesh):
    placed = (
        P(None, ("cuts", "wide", "narrow"), None),
        P(("cuts", "wide"), None, None, None, None),
        P(),
        P(),
    )
    return jax.shard_map(
        local,
        mesh=mesh,
        in_specs=placed,
        out_specs=P(None, ("cuts", "wide", "narrow"), None),
        check_vma=False,
    )
```

```python
import functools

import jax
import jax.numpy as jnp
from jax import lax
from jax.experimental import pallas as pl
from jax.experimental.pallas import tpu as pltpu
from jax.sharding import PartitionSpec as P

F32, BF16, I32 = jnp.float32, jnp.bfloat16, jnp.int32
NN = (((1,), (0,)), ((), ()))
NT = (((1,), (1,)), ((), ()))
LIMIT = 48 * 1024 * 1024
SEND_LIMIT = 61 * 1024 * 1024
KEEP_LIMIT = 48 * 1024 * 1024
CHUNKS_TWO, CHUNKS_FOUR = 2, 1
CUTS_TWO, CUTS_FOUR = 1, 1


def dot(left, right, dims=NN):
    return lax.dot_general(left, right, dims, preferred_element_type=F32)


def complex_dot(lr, li, rr, ri):
    left = jnp.concatenate([lr, li], 1)
    return (
        dot(left, jnp.concatenate([rr, -ri], 0)),
        dot(left, jnp.concatenate([ri, rr], 0)),
    )


def source_of(column, modes_ref, step, modes, permuted):
    total = jnp.zeros_like(column)
    for b in range(modes):
        weight = jnp.left_shift(jnp.int32(1), modes_ref[step, b])
        total = total + jnp.where((column >> b) & 1 == 1, weight, 0)
    return jnp.where(permuted == 1, total, column)


def place():
    w = lax.axis_index("wide")
    return w & 1, w >> 1 & 1, w >> 2, lax.axis_index("narrow")


def steps_of(plan, roots_ref, y, group):
    if plan is not None:
        low, high = (jnp.int32(k) for k in plan)
    else:
        low = high = None
        for k in range(roots_ref.shape[0]):
            mine = roots_ref[k] >> 2 == group
            high = jnp.where(mine, k, 0 if high is None else high)
        for k in reversed(range(roots_ref.shape[0])):
            mine = roots_ref[k] >> 2 == group
            low = jnp.where(mine, k, k if low is None else low)
    return jnp.where(y == 0, low, high), jnp.where(y == 0, high, low)


def send_kernel(plan, roots_ref, modes_ref, leaves_ref, *refs):
    sends, (leaf_ref, sem) = refs[:-2], refs[-2:]
    part, width = sends[0].shape[1:]
    rows = part * len(sends)
    y, zb, group, core = place()
    _, step = steps_of(plan, roots_ref, y, group)

    @pl.when(y == 0)
    def _():
        copies = []
        for i, send_ref in enumerate(sends):
            at = pl.ds(pl.multiple_of(core * rows + i * part, part), part)
            copies.append(
                pltpu.make_async_copy(leaves_ref.at[0, step, :, at], send_ref, sem.at[i])
            )
            copies[-1].start()
        for copy in copies:
            copy.wait()

    @pl.when(y == 1)
    def _():
        copy = pltpu.make_async_copy(leaves_ref.at[0, step], leaf_ref, sem.at[0])
        copy.start()
        column = lax.broadcasted_iota(I32, (rows, 1), 0) + core * rows
        source = source_of(column, modes_ref, step, modes_ref.shape[1], zb)
        picked = lax.broadcasted_iota(I32, (rows, width), 1) == source
        picked = jnp.where(picked, 1.0, 0.0).astype(BF16)
        copy.wait()
        for p in range(2):
            made = dot(picked, leaf_ref[p], NT).astype(BF16)
            for i, send_ref in enumerate(sends):
                send_ref[p] = made[i * part : (i + 1) * part]


def keep_kernel(plan, roots_ref, modes_ref, leaves_ref, keep_ref, leaf_ref, sem):
    width = keep_ref.shape[2]
    y, zb, group, core = place()
    step, _ = steps_of(plan, roots_ref, y, group)
    copy = pltpu.make_async_copy(leaves_ref.at[0, step], leaf_ref, sem.at[0])
    copy.start()
    copy.wait()

    @pl.when(y == 0)
    def _():
        same = lax.broadcasted_iota(I32, (width, width), 0) == lax.broadcasted_iota(
            I32, (width, width), 1
        )
        same = jnp.where(same, 1.0, 0.0).astype(BF16)
        for p in range(2):
            keep_ref[p] = dot(same, leaf_ref[p], NT).astype(BF16)

    @pl.when(y == 1)
    def _():
        column = lax.broadcasted_iota(I32, (1, width), 1)
        source = source_of(column, modes_ref, step, modes_ref.shape[1], zb)
        picked = lax.broadcasted_iota(I32, (width, width), 0) == source
        picked = jnp.where(picked, 1.0, 0.0).astype(BF16)
        for p in range(2):
            keep_ref[p] = dot(leaf_ref[p], picked).astype(BF16)


def leaf_call(kernel, limit, parts, rows, plan, roots, modes, leaves):
    width = leaves.shape[-1]
    return pl.pallas_call(
        functools.partial(kernel, plan),
        grid_spec=pltpu.PrefetchScalarGridSpec(
            num_scalar_prefetch=2,
            grid=(1,),
            in_specs=[pl.BlockSpec(memory_space=pl.ANY)],
            out_specs=[whole((2, rows, width))] * parts,
            scratch_shapes=[pltpu.VMEM((2, width, width), BF16), pltpu.SemaphoreType.DMA((parts,))],
        ),
        out_shape=[jax.ShapeDtypeStruct((2, rows, width), BF16)] * parts,
        compiler_params=pltpu.CompilerParams(vmem_limit_bytes=limit),
    )(roots, modes, leaves)


def whole(shape):
    return pl.BlockSpec(shape, lambda i, *_: (0,) * len(shape))


def call(kernel, arrays, outs):
    return pl.pallas_call(
        kernel,
        grid=(1,),
        in_specs=[whole(a.shape) for a in arrays],
        out_specs=[whole(o.shape) for o in outs],
        out_shape=outs,
        compiler_params=pltpu.CompilerParams(vmem_limit_bytes=LIMIT),
    )(*arrays)


def pair_kernel(left_ref, right_ref, out_ref):
    re, im = complex_dot(left_ref[0], left_ref[1], right_ref[0], right_ref[1])
    out_ref[0] = re.astype(BF16)
    out_ref[1] = im.astype(BF16)


def branch_kernel(chunks, cuts, *refs):
    own, got, own_sib, got_sib = (refs[i * chunks : (i + 1) * chunks] for i in range(4))
    firsts, other_ref = refs[4 * chunks : 4 * chunks + cuts], refs[4 * chunks + cuts]
    y, zb, _, core = place()
    rows, width = own[0].shape[1] * chunks, own[0].shape[2]
    part = rows // 2
    high_here = y == zb

    def joined(group, p, at=slice(None)):
        values = [ref[p, :, at] for ref in group]
        return values[0] if len(values) == 1 else jnp.concatenate(values, 0)

    def multiply(left, near, far):
        re = im = None
        for side, right in ((core, near), (1 - core, far)):
            at = pl.ds(pl.multiple_of(side * rows, rows), rows)
            r, m = complex_dot(
                joined(left, 0, at), joined(left, 1, at), joined(right, 0), joined(right, 1)
            )
            re, im = (r, m) if re is None else (re + r, im + m)
        return re.astype(BF16), im.astype(BF16)

    def store(p, top, bottom):
        for here, first, second in ((0, top, bottom), (1, bottom, top)):

            @pl.when(zb == here)
            def _():
                for i, ref in enumerate(firsts):
                    ref[p] = first[i * part // cuts : (i + 1) * part // cuts]
                if len(other_ref.shape) == 4:
                    other_ref[0, p] = first
                    other_ref[1, p] = second
                else:
                    other_ref[p] = second

    def finish(parts):
        @pl.when(y == 1)
        def _():
            for p, value in enumerate(parts):
                store(p, value[:part], value[part:])

        @pl.when(y == 0)
        def _():
            same = lax.broadcasted_iota(I32, (rows, rows), 0) == lax.broadcasted_iota(
                I32, (rows, rows), 1
            )
            same = jnp.where(same, 1.0, 0.0).astype(BF16)
            for p, value in enumerate(parts):
                turned = [dot(same, value[:, i : i + rows], NT) for i in range(0, width, rows)]
                both = jnp.concatenate(turned, 1).astype(BF16)
                store(p, both[:part], both[part:])

    @pl.when(high_here)
    def _():
        finish(multiply(got, own, own_sib))

    @pl.when(jnp.logical_not(high_here))
    def _():
        finish(multiply(own, got, got_sib))


def stem_kernel(plans, turn, layout, roots_ref, own_hbm, sib_hbm, *refs):
    pieces, (out_hbm, o_ref, n1_ref, own_ref, sib_ref, out_ref, sem) = refs[:-7], refs[-7:]
    items = 4
    y, zb, group, core = place()
    zb = zb if turn else 0
    width = own_hbm.shape[2]
    half = width // 2
    part = half // 2
    first = [
        pltpu.make_async_copy(own_hbm, own_ref, sem.at[items]),
        pltpu.make_async_copy(sib_hbm, sib_ref, sem.at[items + 1]),
    ]
    for copy in first:
        copy.start()
    for m in range(items):
        plan = plans[m // 2] if plans else None
        steps = steps_of(plan, roots_ref, y, group if m < 2 else 1 - group)
        step = steps[m % 2]
        column = y if m % 2 == 0 else 1 - y
        for ref, (item, far, halves) in zip(pieces, layout):
            if item != m:
                continue
            side = 1 - core if far else core
            for h, offset in halves:
                source = ref if len(halves) == 1 else ref.at[h]
                count = source.shape[1]
                for s in range(2):
                    row = jnp.where(column == 1, side, s) * half + offset
                    row = row + (1 - zb if h else zb) * part
                    col = jnp.where(column == 1, s, side) * half
                    pltpu.make_async_copy(
                        source.at[:, :, s * half : (s + 1) * half],
                        o_ref.at[
                            step,
                            :,
                            pl.ds(pl.multiple_of(row, count), count),
                            pl.ds(pl.multiple_of(col, half), half),
                        ],
                        sem.at[step],
                    ).start()

    def arrived(step):
        pltpu.make_async_copy(o_ref.at[step], o_ref.at[step], sem.at[step]).wait()

    for copy in first:
        copy.wait()
    arrived(0)
    for f, ref in ((core, own_ref), (1 - core, sib_ref)):
        at = pl.ds(pl.multiple_of(f * half, half), half)
        t = complex_dot(ref[0], ref[1], o_ref[0, 0], o_ref[0, 1])
        for p in range(2):
            value = t[p].astype(BF16)
            for e in range(2):
                n1_ref[e, p, :, at] = value[:, e * half : (e + 1) * half]
    mine = pl.ds(pl.multiple_of(core * half, half), half)
    arrived(1)
    arrived(2)
    o12 = complex_dot(o_ref[1, 0], o_ref[1, 1], o_ref[2, 0, :, mine], o_ref[2, 1, :, mine])
    o12 = [v.astype(BF16) for v in o12]
    arrived(3)
    rows = own_ref.shape[1]
    copies = []
    for r in range(2):
        band = slice(r * rows // 2, (r + 1) * rows // 2)
        n4 = [complex_dot(n1_ref[e, 0, band], n1_ref[e, 1, band], *o12) for e in range(2)]
        n4 = [jnp.concatenate([n4[0][p], n4[1][p]], 1).astype(BF16) for p in range(2)]
        made = complex_dot(*n4, o_ref[3, 0], o_ref[3, 1])
        for p in range(2):
            out_ref[p, band] = made[p]
        copy = pltpu.make_async_copy(
            out_ref.at[:, band], out_hbm.at[:, band], sem.at[items + 2 + r]
        )
        copy.start()
        copies.append(copy)
    for copy in copies:
        copy.wait()


def stem_call(plans, turn, roots, own, sib, items):
    shape = own.shape
    width = shape[2]
    pieces, layout = [], []
    for m, item in enumerate(items):
        for array, far, halves in item:
            pieces.append(array)
            layout.append((m, far, halves))
    anywhere = pl.BlockSpec(memory_space=pl.ANY)
    return pl.pallas_call(
        functools.partial(stem_kernel, plans, turn, tuple(layout)),
        grid_spec=pltpu.PrefetchScalarGridSpec(
            num_scalar_prefetch=1,
            grid=(1,),
            in_specs=[anywhere] * (2 + len(pieces)),
            out_specs=anywhere,
            scratch_shapes=[
                pltpu.VMEM((len(items), 2, width, width), BF16),
                pltpu.VMEM((2, *shape), BF16),
                pltpu.VMEM(shape, BF16),
                pltpu.VMEM(shape, BF16),
                pltpu.VMEM(shape, F32),
                pltpu.SemaphoreType.DMA((len(items) + 4,)),
            ],
        ),
        out_shape=jax.ShapeDtypeStruct(shape, F32),
        compiler_params=pltpu.CompilerParams(vmem_limit_bytes=LIMIT),
    )(roots, own, sib, *pieces)


def swap(value, axis, bit):
    n = lax.axis_size(axis)
    return lax.ppermute(value, axis, [(i, i ^ bit) for i in range(n)])


def other_core(value):
    return swap(value, "narrow", 1)


def select_kernel(plan, roots_ref, made_ref, other_ref, out_ref):
    y, _, group, _ = place()
    step, _ = steps_of(plan, roots_ref, y, group)
    owned = roots_ref[step] >> 2 == group

    @pl.when(owned)
    def _():
        out_ref[...] = made_ref[...]

    @pl.when(jnp.logical_not(owned))
    def _():
        out_ref[...] = other_ref[...]


def select_call(plan, roots, made, other):
    return pl.pallas_call(
        functools.partial(select_kernel, plan),
        grid_spec=pltpu.PrefetchScalarGridSpec(
            num_scalar_prefetch=1,
            grid=(1,),
            in_specs=[whole(made.shape)] * 2,
            out_specs=whole(made.shape),
        ),
        out_shape=jax.ShapeDtypeStruct(made.shape, made.dtype),
        compiler_params=pltpu.CompilerParams(vmem_limit_bytes=LIMIT),
    )(roots, made, other)


def tree(leaves, roots, modes, plan, chunks, joint, cuts):
    width = leaves.shape[-1]
    rows = width // lax.axis_size("narrow")
    sends = leaf_call(send_kernel, SEND_LIMIT, chunks, rows // chunks, plan, roots, modes, leaves)
    [keep] = leaf_call(keep_kernel, KEEP_LIMIT, 1, width, plan, roots, modes, leaves)
    lefts = [swap(send, "wide", 1) for send in sends]
    pairs = [
        call(pair_kernel, [left, keep], [jax.ShapeDtypeStruct(left.shape, BF16)])[0]
        for left in lefts
    ]
    gots = [swap(pair, "wide", 2) for pair in pairs]
    sibs = [other_core(v) for v in pairs + gots]
    piece = jax.ShapeDtypeStruct((2, rows // 2, width), BF16)
    cut = jax.ShapeDtypeStruct((2, rows // 2 // cuts, width), BF16)
    other = jax.ShapeDtypeStruct((2, *piece.shape), BF16) if joint else piece
    made = call(
        functools.partial(branch_kernel, chunks, cuts), pairs + gots + sibs, [cut] * cuts + [other]
    )
    return made[:-1], made[-1]


def item_of(firsts, seconds):
    item = []
    for half, group in enumerate((firsts, seconds)):
        for i, piece in enumerate(group):
            place_of = ((half, i * piece.shape[1]),)
            item += [(piece, False, place_of), (other_core(piece), True, place_of)]
    return item


def joint_item(both):
    place_of = ((0, 0), (1, 0))
    return [(both, False, place_of), (other_core(both), True, place_of)]


def all_swapped(values, bit):
    return [swap(value, "wide", bit) for value in values]


def each_own_two(stem, leaves, roots, modes):
    own = stem.astype(BF16)
    sib = other_core(own)
    firsts, both = tree(leaves, roots, modes, None, CHUNKS_TWO, True, CUTS_TWO)
    far = all_swapped(firsts, 4)
    near = [joint_item(both), joint_item(swap(both, "wide", 1))]
    far_second = all_swapped(far, 2)
    away = [item_of(far, far_second), item_of(all_swapped(far, 1), all_swapped(far_second, 1))]
    return stem_call(None, True, roots, own, sib, near + away)


def any_owners(stem, leaves, roots, modes):
    y, zb, group, _ = place()
    own = stem.astype(BF16)
    sib = other_core(own)
    two = lax.axis_size("wide") == 8
    items, plans = [], []
    for j in range(leaves.shape[1] // 2):
        plan = (2 * j, 2 * j + 1)
        firsts, second = tree(
            leaves, roots, modes, plan, CHUNKS_FOUR, False, CUTS_FOUR if two else 1
        )
        owned = roots[2 * j + y] // 4 == group
        if two:
            here = [select_call(plan, roots, v, swap(v, "wide", 4)) for v in firsts]
            seconds = all_swapped(here, 2)
            cross = [all_swapped(here, 1), all_swapped(seconds, 1)]
        else:
            sums = [
                lax.psum(
                    jnp.where(owned & (zb == 0) & (y == side), v, jnp.zeros_like(v)), "wide"
                )
                for side in range(2)
                for v in (firsts[0], second)
            ]
            here, seconds = ([jnp.where(y == 0, a, b)] for a, b in zip(sums[:2], sums[2:]))
            cross = [[jnp.where(y == 0, b, a)] for a, b in zip(sums[:2], sums[2:])]
        items += [item_of(here, seconds), item_of(*cross)]
        plans.append(plan)
    return stem_call(tuple(plans), two, roots, own, sib, items)


MODE = "cond"


def local(stem_tensor, leaves, root_devices, mode_orders):
    given = (stem_tensor, leaves, root_devices, mode_orders)
    if lax.axis_size("wide") != 8 or MODE == "four":
        return any_owners(*given)
    if MODE == "two":
        return each_own_two(*given)
    return lax.cond(jnp.sum(root_devices // 4) == 2, each_own_two, any_owners, *given)


def solution(mesh):
    placed = (
        P(None, ("cuts", "wide", "narrow"), None),
        P(("cuts", "wide"), None, None, None, None),
        P(),
        P(),
    )
    return jax.shard_map(
        local,
        mesh=mesh,
        in_specs=placed,
        out_specs=P(None, ("cuts", "wide", "narrow"), None),
        check_vma=False,
    )
```

```python
import functools

import jax
import jax.numpy as jnp
from jax import lax
from jax.experimental import pallas as pl
from jax.experimental.pallas import tpu as pltpu
from jax.sharding import PartitionSpec as P

F32, BF16, I32 = jnp.float32, jnp.bfloat16, jnp.int32
NN = (((1,), (0,)), ((), ()))
NT = (((1,), (1,)), ((), ()))
LIMIT = 48 * 1024 * 1024
SEND_LIMIT = 61 * 1024 * 1024
KEEP_LIMIT = 48 * 1024 * 1024
CHUNKS_TWO, CHUNKS_FOUR = 2, 2
CUTS_TWO, CUTS_FOUR = 1, 1


def dot(left, right, dims=NN):
    return lax.dot_general(left, right, dims, preferred_element_type=F32)


def complex_dot(lr, li, rr, ri):
    left = jnp.concatenate([lr, li], 1)
    return (
        dot(left, jnp.concatenate([rr, -ri], 0)),
        dot(left, jnp.concatenate([ri, rr], 0)),
    )


def source_of(column, modes_ref, step, modes, permuted):
    total = jnp.zeros_like(column)
    for b in range(modes):
        weight = jnp.left_shift(jnp.int32(1), modes_ref[step, b])
        total = total + jnp.where((column >> b) & 1 == 1, weight, 0)
    return jnp.where(permuted == 1, total, column)


def place():
    w = lax.axis_index("wide")
    return w & 1, w >> 1 & 1, w >> 2, lax.axis_index("narrow")


def steps_of(plan, roots_ref, y, group):
    if plan is not None:
        low, high = (jnp.int32(k) for k in plan)
    else:
        low = high = None
        for k in range(roots_ref.shape[0]):
            mine = roots_ref[k] >> 2 == group
            high = jnp.where(mine, k, 0 if high is None else high)
        for k in reversed(range(roots_ref.shape[0])):
            mine = roots_ref[k] >> 2 == group
            low = jnp.where(mine, k, k if low is None else low)
    return jnp.where(y == 0, low, high), jnp.where(y == 0, high, low)


def send_kernel(plan, roots_ref, modes_ref, leaves_ref, *refs):
    sends, (leaf_ref, sem) = refs[:-2], refs[-2:]
    part, width = sends[0].shape[1:]
    rows = part * len(sends)
    y, zb, group, core = place()
    _, step = steps_of(plan, roots_ref, y, group)

    @pl.when(y == 0)
    def _():
        copies = []
        for i, send_ref in enumerate(sends):
            at = pl.ds(pl.multiple_of(core * rows + i * part, part), part)
            copies.append(
                pltpu.make_async_copy(leaves_ref.at[0, step, :, at], send_ref, sem.at[i])
            )
            copies[-1].start()
        for copy in copies:
            copy.wait()

    @pl.when(y == 1)
    def _():
        copy = pltpu.make_async_copy(leaves_ref.at[0, step], leaf_ref, sem.at[0])
        copy.start()
        column = lax.broadcasted_iota(I32, (rows, 1), 0) + core * rows
        source = source_of(column, modes_ref, step, modes_ref.shape[1], zb)
        picked = lax.broadcasted_iota(I32, (rows, width), 1) == source
        picked = jnp.where(picked, 1.0, 0.0).astype(BF16)
        copy.wait()
        for p in range(2):
            made = dot(picked, leaf_ref[p], NT).astype(BF16)
            for i, send_ref in enumerate(sends):
                send_ref[p] = made[i * part : (i + 1) * part]


def keep_kernel(plan, roots_ref, modes_ref, leaves_ref, keep_ref, leaf_ref, sem):
    width = keep_ref.shape[2]
    y, zb, group, core = place()
    step, _ = steps_of(plan, roots_ref, y, group)
    copy = pltpu.make_async_copy(leaves_ref.at[0, step], leaf_ref, sem.at[0])
    copy.start()
    copy.wait()

    @pl.when(y == 0)
    def _():
        same = lax.broadcasted_iota(I32, (width, width), 0) == lax.broadcasted_iota(
            I32, (width, width), 1
        )
        same = jnp.where(same, 1.0, 0.0).astype(BF16)
        for p in range(2):
            keep_ref[p] = dot(same, leaf_ref[p], NT).astype(BF16)

    @pl.when(y == 1)
    def _():
        column = lax.broadcasted_iota(I32, (1, width), 1)
        source = source_of(column, modes_ref, step, modes_ref.shape[1], zb)
        picked = lax.broadcasted_iota(I32, (width, width), 0) == source
        picked = jnp.where(picked, 1.0, 0.0).astype(BF16)
        for p in range(2):
            keep_ref[p] = dot(leaf_ref[p], picked).astype(BF16)


def leaf_call(kernel, limit, parts, rows, plan, roots, modes, leaves):
    width = leaves.shape[-1]
    return pl.pallas_call(
        functools.partial(kernel, plan),
        grid_spec=pltpu.PrefetchScalarGridSpec(
            num_scalar_prefetch=2,
            grid=(1,),
            in_specs=[pl.BlockSpec(memory_space=pl.ANY)],
            out_specs=[whole((2, rows, width))] * parts,
            scratch_shapes=[pltpu.VMEM((2, width, width), BF16), pltpu.SemaphoreType.DMA((parts,))],
        ),
        out_shape=[jax.ShapeDtypeStruct((2, rows, width), BF16)] * parts,
        compiler_params=pltpu.CompilerParams(vmem_limit_bytes=limit),
    )(roots, modes, leaves)


def whole(shape):
    return pl.BlockSpec(shape, lambda i, *_: (0,) * len(shape))


def call(kernel, arrays, outs):
    return pl.pallas_call(
        kernel,
        grid=(1,),
        in_specs=[whole(a.shape) for a in arrays],
        out_specs=[whole(o.shape) for o in outs],
        out_shape=outs,
        compiler_params=pltpu.CompilerParams(vmem_limit_bytes=LIMIT),
    )(*arrays)


def pair_kernel(left_ref, right_ref, out_ref):
    re, im = complex_dot(left_ref[0], left_ref[1], right_ref[0], right_ref[1])
    out_ref[0] = re.astype(BF16)
    out_ref[1] = im.astype(BF16)


def branch_kernel(chunks, cuts, *refs):
    own, got, own_sib, got_sib = (refs[i * chunks : (i + 1) * chunks] for i in range(4))
    firsts, other_ref = refs[4 * chunks : 4 * chunks + cuts], refs[4 * chunks + cuts]
    y, zb, _, core = place()
    rows, width = own[0].shape[1] * chunks, own[0].shape[2]
    part = rows // 2
    high_here = y == zb

    def joined(group, p, at=slice(None)):
        values = [ref[p, :, at] for ref in group]
        return values[0] if len(values) == 1 else jnp.concatenate(values, 0)

    def multiply(left, near, far):
        re = im = None
        for side, right in ((core, near), (1 - core, far)):
            at = pl.ds(pl.multiple_of(side * rows, rows), rows)
            r, m = complex_dot(
                joined(left, 0, at), joined(left, 1, at), joined(right, 0), joined(right, 1)
            )
            re, im = (r, m) if re is None else (re + r, im + m)
        return re.astype(BF16), im.astype(BF16)

    def store(p, top, bottom):
        for here, first, second in ((0, top, bottom), (1, bottom, top)):

            @pl.when(zb == here)
            def _():
                for i, ref in enumerate(firsts):
                    ref[p] = first[i * part // cuts : (i + 1) * part // cuts]
                if len(other_ref.shape) == 4:
                    other_ref[0, p] = first
                    other_ref[1, p] = second
                else:
                    other_ref[p] = second

    def finish(parts):
        @pl.when(y == 1)
        def _():
            for p, value in enumerate(parts):
                store(p, value[:part], value[part:])

        @pl.when(y == 0)
        def _():
            same = lax.broadcasted_iota(I32, (rows, rows), 0) == lax.broadcasted_iota(
                I32, (rows, rows), 1
            )
            same = jnp.where(same, 1.0, 0.0).astype(BF16)
            for p, value in enumerate(parts):
                turned = [dot(same, value[:, i : i + rows], NT) for i in range(0, width, rows)]
                both = jnp.concatenate(turned, 1).astype(BF16)
                store(p, both[:part], both[part:])

    @pl.when(high_here)
    def _():
        finish(multiply(got, own, own_sib))

    @pl.when(jnp.logical_not(high_here))
    def _():
        finish(multiply(own, got, got_sib))


def stem_kernel(plans, turn, layout, roots_ref, own_hbm, sib_hbm, *refs):
    pieces, (out_hbm, o_ref, n1_ref, own_ref, sib_ref, out_ref, sem) = refs[:-7], refs[-7:]
    items = 4
    y, zb, group, core = place()
    zb = zb if turn else 0
    width = own_hbm.shape[2]
    half = width // 2
    part = half // 2
    first = [
        pltpu.make_async_copy(own_hbm, own_ref, sem.at[items]),
        pltpu.make_async_copy(sib_hbm, sib_ref, sem.at[items + 1]),
    ]
    for copy in first:
        copy.start()
    for m in range(items):
        plan = plans[m // 2] if plans else None
        steps = steps_of(plan, roots_ref, y, group if m < 2 else 1 - group)
        step = steps[m % 2]
        column = y if m % 2 == 0 else 1 - y
        for ref, (item, far, halves) in zip(pieces, layout):
            if item != m:
                continue
            side = 1 - core if far else core
            for h, offset in halves:
                source = ref if len(halves) == 1 else ref.at[h]
                count = source.shape[1]
                for s in range(2):
                    row = jnp.where(column == 1, side, s) * half + offset
                    row = row + (1 - zb if h else zb) * part
                    col = jnp.where(column == 1, s, side) * half
                    pltpu.make_async_copy(
                        source.at[:, :, s * half : (s + 1) * half],
                        o_ref.at[
                            step,
                            :,
                            pl.ds(pl.multiple_of(row, count), count),
                            pl.ds(pl.multiple_of(col, half), half),
                        ],
                        sem.at[step],
                    ).start()

    def arrived(step):
        pltpu.make_async_copy(o_ref.at[step], o_ref.at[step], sem.at[step]).wait()

    for copy in first:
        copy.wait()
    arrived(0)
    for f, ref in ((core, own_ref), (1 - core, sib_ref)):
        at = pl.ds(pl.multiple_of(f * half, half), half)
        t = complex_dot(ref[0], ref[1], o_ref[0, 0], o_ref[0, 1])
        for p in range(2):
            value = t[p].astype(BF16)
            for e in range(2):
                n1_ref[e, p, :, at] = value[:, e * half : (e + 1) * half]
    mine = pl.ds(pl.multiple_of(core * half, half), half)
    arrived(1)
    arrived(2)
    o12 = complex_dot(o_ref[1, 0], o_ref[1, 1], o_ref[2, 0, :, mine], o_ref[2, 1, :, mine])
    o12 = [v.astype(BF16) for v in o12]
    arrived(3)
    rows = own_ref.shape[1]
    copies = []
    for r in range(2):
        band = slice(r * rows // 2, (r + 1) * rows // 2)
        n4 = [complex_dot(n1_ref[e, 0, band], n1_ref[e, 1, band], *o12) for e in range(2)]
        n4 = [jnp.concatenate([n4[0][p], n4[1][p]], 1).astype(BF16) for p in range(2)]
        made = complex_dot(*n4, o_ref[3, 0], o_ref[3, 1])
        for p in range(2):
            out_ref[p, band] = made[p]
        copy = pltpu.make_async_copy(
            out_ref.at[:, band], out_hbm.at[:, band], sem.at[items + 2 + r]
        )
        copy.start()
        copies.append(copy)
    for copy in copies:
        copy.wait()


def stem_call(plans, turn, roots, own, sib, items):
    shape = own.shape
    width = shape[2]
    pieces, layout = [], []
    for m, item in enumerate(items):
        for array, far, halves in item:
            pieces.append(array)
            layout.append((m, far, halves))
    anywhere = pl.BlockSpec(memory_space=pl.ANY)
    return pl.pallas_call(
        functools.partial(stem_kernel, plans, turn, tuple(layout)),
        grid_spec=pltpu.PrefetchScalarGridSpec(
            num_scalar_prefetch=1,
            grid=(1,),
            in_specs=[anywhere] * (2 + len(pieces)),
            out_specs=anywhere,
            scratch_shapes=[
                pltpu.VMEM((len(items), 2, width, width), BF16),
                pltpu.VMEM((2, *shape), BF16),
                pltpu.VMEM(shape, BF16),
                pltpu.VMEM(shape, BF16),
                pltpu.VMEM(shape, F32),
                pltpu.SemaphoreType.DMA((len(items) + 4,)),
            ],
        ),
        out_shape=jax.ShapeDtypeStruct(shape, F32),
        compiler_params=pltpu.CompilerParams(vmem_limit_bytes=LIMIT),
    )(roots, own, sib, *pieces)


def swap(value, axis, bit):
    n = lax.axis_size(axis)
    return lax.ppermute(value, axis, [(i, i ^ bit) for i in range(n)])


def other_core(value):
    return swap(value, "narrow", 1)


def select_kernel(plan, roots_ref, made_ref, other_ref, out_ref):
    y, _, group, _ = place()
    step, _ = steps_of(plan, roots_ref, y, group)
    owned = roots_ref[step] >> 2 == group

    @pl.when(owned)
    def _():
        out_ref[...] = made_ref[...]

    @pl.when(jnp.logical_not(owned))
    def _():
        out_ref[...] = other_ref[...]


def select_call(plan, roots, made, other):
    return pl.pallas_call(
        functools.partial(select_kernel, plan),
        grid_spec=pltpu.PrefetchScalarGridSpec(
            num_scalar_prefetch=1,
            grid=(1,),
            in_specs=[whole(made.shape)] * 2,
            out_specs=whole(made.shape),
        ),
        out_shape=jax.ShapeDtypeStruct(made.shape, made.dtype),
        compiler_params=pltpu.CompilerParams(vmem_limit_bytes=LIMIT),
    )(roots, made, other)


def after(value, other):
    return lax.optimization_barrier((value, other))[0]


def sends_of(leaves, roots, modes, plan, chunks):
    rows = leaves.shape[-1] // lax.axis_size("narrow")
    return leaf_call(send_kernel, SEND_LIMIT, chunks, rows // chunks, plan, roots, modes, leaves)


def tree(leaves, roots, modes, plan, sends, joint, cuts, ahead=None, sent=None):
    width = leaves.shape[-1]
    rows = width // lax.axis_size("narrow")
    chunks = len(sends)
    if sent is not None:
        leaves = after(leaves, sent)
    [keep] = leaf_call(keep_kernel, KEEP_LIMIT, 1, width, plan, roots, modes, leaves)
    lefts = [swap(send, "wide", 1) for send in sends]
    pairs = [
        call(pair_kernel, [left, keep], [jax.ShapeDtypeStruct(left.shape, BF16)])[0]
        for left in lefts
    ]
    gots = [swap(pair, "wide", 2) for pair in pairs]
    held = gots if ahead is None else [after(got, ahead) for got in gots]
    sibs = [other_core(v) for v in pairs + held]
    piece = jax.ShapeDtypeStruct((2, rows // 2, width), BF16)
    cut = jax.ShapeDtypeStruct((2, rows // 2 // cuts, width), BF16)
    other = jax.ShapeDtypeStruct((2, *piece.shape), BF16) if joint else piece
    made = call(
        functools.partial(branch_kernel, chunks, cuts), pairs + gots + sibs, [cut] * cuts + [other]
    )
    return made[:-1], made[-1]


def item_of(firsts, seconds):
    item = []
    for half, group in enumerate((firsts, seconds)):
        for i, piece in enumerate(group):
            place_of = ((half, i * piece.shape[1]),)
            item += [(piece, False, place_of), (other_core(piece), True, place_of)]
    return item


def joint_item(both):
    place_of = ((0, 0), (1, 0))
    return [(both, False, place_of), (other_core(both), True, place_of)]


def all_swapped(values, bit):
    return [swap(value, "wide", bit) for value in values]


def each_own_two(stem, leaves, roots, modes):
    own = stem.astype(BF16)
    sib = other_core(own)
    firsts, both = tree(
        leaves, roots, modes, None, sends_of(leaves, roots, modes, None, CHUNKS_TWO), True, CUTS_TWO
    )
    far = all_swapped(firsts, 4)
    near = [joint_item(both), joint_item(swap(both, "wide", 1))]
    far_second = all_swapped(far, 2)
    away = [item_of(far, far_second), item_of(all_swapped(far, 1), all_swapped(far_second, 1))]
    return stem_call(None, True, roots, own, sib, near + away)


def any_owners(stem, leaves, roots, modes):
    y, zb, group, _ = place()
    own = stem.astype(BF16)
    sib = other_core(own)
    two = lax.axis_size("wide") == 8
    items, plans, ahead = [], [], None
    every = [(k, k + 1) for k in range(0, leaves.shape[1], 2)]
    sends = [sends_of(leaves, roots, modes, plan, CHUNKS_FOUR) for plan in every]
    for j, plan in enumerate(every):
        firsts, second = tree(
            leaves,
            roots,
            modes,
            plan,
            sends[j],
            False,
            CUTS_FOUR if two else 1,
            ahead,
            sends[1][0] if j == 0 else None,
        )
        owned = roots[2 * j + y] // 4 == group
        if two:
            crossed = all_swapped(firsts, 4)
            ahead = crossed[0]
            here = [select_call(plan, roots, v, c) for v, c in zip(firsts, crossed)]
            seconds = all_swapped(here, 2)
            cross = [all_swapped(here, 1), all_swapped(seconds, 1)]
        else:
            sums = [
                lax.psum(
                    jnp.where(owned & (zb == 0) & (y == side), v, jnp.zeros_like(v)), "wide"
                )
                for side in range(2)
                for v in (firsts[0], second)
            ]
            here, seconds = ([jnp.where(y == 0, a, b)] for a, b in zip(sums[:2], sums[2:]))
            cross = [[jnp.where(y == 0, b, a)] for a, b in zip(sums[:2], sums[2:])]
        items += [item_of(here, seconds), item_of(*cross)]
        plans.append(plan)
    return stem_call(tuple(plans), two, roots, own, sib, items)


MODE = "cond"


def local(stem_tensor, leaves, root_devices, mode_orders):
    given = (stem_tensor, leaves, root_devices, mode_orders)
    if lax.axis_size("wide") != 8 or MODE == "four":
        return any_owners(*given)
    if MODE == "two":
        return each_own_two(*given)
    return lax.cond(jnp.sum(root_devices // 4) == 2, each_own_two, any_owners, *given)


def solution(mesh):
    placed = (
        P(None, ("cuts", "wide", "narrow"), None),
        P(("cuts", "wide"), None, None, None, None),
        P(),
        P(),
    )
    return jax.shard_map(
        local,
        mesh=mesh,
        in_specs=placed,
        out_specs=P(None, ("cuts", "wide", "narrow"), None),
        check_vma=False,
    )
```

```python
import functools

import jax
import jax.numpy as jnp
from jax import lax
from jax.experimental import pallas as pl
from jax.experimental.pallas import tpu as pltpu
from jax.sharding import PartitionSpec as P

F32, BF16, I32 = jnp.float32, jnp.bfloat16, jnp.int32
NN = (((1,), (0,)), ((), ()))
NT = (((1,), (1,)), ((), ()))
LIMIT = 48 * 1024 * 1024
SEND_LIMIT = 61 * 1024 * 1024
KEEP_LIMIT = 48 * 1024 * 1024
CHUNKS_TWO, CHUNKS_FOUR = 2, 2
CUTS_TWO, CUTS_FOUR = 1, 1


def dot(left, right, dims=NN):
    return lax.dot_general(left, right, dims, preferred_element_type=F32)


def complex_dot(lr, li, rr, ri):
    left = jnp.concatenate([lr, li], 1)
    return (
        dot(left, jnp.concatenate([rr, -ri], 0)),
        dot(left, jnp.concatenate([ri, rr], 0)),
    )


def source_of(column, modes_ref, step, modes, permuted):
    total = jnp.zeros_like(column)
    for b in range(modes):
        weight = jnp.left_shift(jnp.int32(1), modes_ref[step, b])
        total = total + jnp.where((column >> b) & 1 == 1, weight, 0)
    return jnp.where(permuted == 1, total, column)


def place():
    w = lax.axis_index("wide")
    return w & 1, w >> 1 & 1, w >> 2, lax.axis_index("narrow")


def steps_of(plan, roots_ref, y, group):
    if plan is not None:
        low, high = (jnp.int32(k) for k in plan)
    else:
        low = high = None
        for k in range(roots_ref.shape[0]):
            mine = roots_ref[k] >> 2 == group
            high = jnp.where(mine, k, 0 if high is None else high)
        for k in reversed(range(roots_ref.shape[0])):
            mine = roots_ref[k] >> 2 == group
            low = jnp.where(mine, k, k if low is None else low)
    return jnp.where(y == 0, low, high), jnp.where(y == 0, high, low)


def send_kernel(plan, roots_ref, modes_ref, leaves_ref, *refs):
    sends, (leaf_ref, sem) = refs[:-2], refs[-2:]
    part, width = sends[0].shape[1:]
    rows = part * len(sends)
    y, zb, group, core = place()
    _, step = steps_of(plan, roots_ref, y, group)

    @pl.when(y == 0)
    def _():
        copies = []
        for i, send_ref in enumerate(sends):
            at = pl.ds(pl.multiple_of(core * rows + i * part, part), part)
            copies.append(
                pltpu.make_async_copy(leaves_ref.at[0, step, :, at], send_ref, sem.at[i])
            )
            copies[-1].start()
        for copy in copies:
            copy.wait()

    @pl.when(y == 1)
    def _():
        copy = pltpu.make_async_copy(leaves_ref.at[0, step], leaf_ref, sem.at[0])
        copy.start()
        column = lax.broadcasted_iota(I32, (rows, 1), 0) + core * rows
        source = source_of(column, modes_ref, step, modes_ref.shape[1], zb)
        picked = lax.broadcasted_iota(I32, (rows, width), 1) == source
        picked = jnp.where(picked, 1.0, 0.0).astype(BF16)
        copy.wait()
        for p in range(2):
            made = dot(picked, leaf_ref[p], NT).astype(BF16)
            for i, send_ref in enumerate(sends):
                send_ref[p] = made[i * part : (i + 1) * part]


def keep_kernel(plan, roots_ref, modes_ref, leaves_ref, keep_ref, leaf_ref, sem):
    width = keep_ref.shape[2]
    y, zb, group, core = place()
    step, _ = steps_of(plan, roots_ref, y, group)
    copy = pltpu.make_async_copy(leaves_ref.at[0, step], leaf_ref, sem.at[0])
    copy.start()
    copy.wait()

    @pl.when(y == 0)
    def _():
        same = lax.broadcasted_iota(I32, (width, width), 0) == lax.broadcasted_iota(
            I32, (width, width), 1
        )
        same = jnp.where(same, 1.0, 0.0).astype(BF16)
        for p in range(2):
            keep_ref[p] = dot(same, leaf_ref[p], NT).astype(BF16)

    @pl.when(y == 1)
    def _():
        column = lax.broadcasted_iota(I32, (1, width), 1)
        source = source_of(column, modes_ref, step, modes_ref.shape[1], zb)
        picked = lax.broadcasted_iota(I32, (width, width), 0) == source
        picked = jnp.where(picked, 1.0, 0.0).astype(BF16)
        for p in range(2):
            keep_ref[p] = dot(leaf_ref[p], picked).astype(BF16)


def leaf_call(kernel, limit, parts, rows, plan, roots, modes, leaves):
    width = leaves.shape[-1]
    return pl.pallas_call(
        functools.partial(kernel, plan),
        grid_spec=pltpu.PrefetchScalarGridSpec(
            num_scalar_prefetch=2,
            grid=(1,),
            in_specs=[pl.BlockSpec(memory_space=pl.ANY)],
            out_specs=[whole((2, rows, width))] * parts,
            scratch_shapes=[pltpu.VMEM((2, width, width), BF16), pltpu.SemaphoreType.DMA((parts,))],
        ),
        out_shape=[jax.ShapeDtypeStruct((2, rows, width), BF16)] * parts,
        compiler_params=pltpu.CompilerParams(vmem_limit_bytes=limit),
    )(roots, modes, leaves)


def whole(shape):
    return pl.BlockSpec(shape, lambda i, *_: (0,) * len(shape))


def call(kernel, arrays, outs):
    return pl.pallas_call(
        kernel,
        grid=(1,),
        in_specs=[whole(a.shape) for a in arrays],
        out_specs=[whole(o.shape) for o in outs],
        out_shape=outs,
        compiler_params=pltpu.CompilerParams(vmem_limit_bytes=LIMIT),
    )(*arrays)


def pair_kernel(left_ref, right_ref, out_ref):
    re, im = complex_dot(left_ref[0], left_ref[1], right_ref[0], right_ref[1])
    out_ref[0] = re.astype(BF16)
    out_ref[1] = im.astype(BF16)


def branch_kernel(chunks, cuts, *refs):
    own, got, own_sib, got_sib = (refs[i * chunks : (i + 1) * chunks] for i in range(4))
    firsts, other_ref = refs[4 * chunks : 4 * chunks + cuts], refs[4 * chunks + cuts]
    y, zb, _, core = place()
    rows, width = own[0].shape[1] * chunks, own[0].shape[2]
    part = rows // 2
    high_here = y == zb

    def joined(group, p, at=slice(None)):
        values = [ref[p, :, at] for ref in group]
        return values[0] if len(values) == 1 else jnp.concatenate(values, 0)

    def multiply(left, near, far):
        re = im = None
        for side, right in ((core, near), (1 - core, far)):
            at = pl.ds(pl.multiple_of(side * rows, rows), rows)
            r, m = complex_dot(
                joined(left, 0, at), joined(left, 1, at), joined(right, 0), joined(right, 1)
            )
            re, im = (r, m) if re is None else (re + r, im + m)
        return re.astype(BF16), im.astype(BF16)

    def store(p, top, bottom):
        for here, first, second in ((0, top, bottom), (1, bottom, top)):

            @pl.when(zb == here)
            def _():
                for i, ref in enumerate(firsts):
                    ref[p] = first[i * part // cuts : (i + 1) * part // cuts]
                if len(other_ref.shape) == 4:
                    other_ref[0, p] = first
                    other_ref[1, p] = second
                else:
                    other_ref[p] = second

    def finish(parts):
        @pl.when(y == 1)
        def _():
            for p, value in enumerate(parts):
                store(p, value[:part], value[part:])

        @pl.when(y == 0)
        def _():
            same = lax.broadcasted_iota(I32, (rows, rows), 0) == lax.broadcasted_iota(
                I32, (rows, rows), 1
            )
            same = jnp.where(same, 1.0, 0.0).astype(BF16)
            for p, value in enumerate(parts):
                turned = [dot(same, value[:, i : i + rows], NT) for i in range(0, width, rows)]
                both = jnp.concatenate(turned, 1).astype(BF16)
                store(p, both[:part], both[part:])

    @pl.when(high_here)
    def _():
        finish(multiply(got, own, own_sib))

    @pl.when(jnp.logical_not(high_here))
    def _():
        finish(multiply(own, got, got_sib))


def stem_kernel(plans, turn, layout, roots_ref, own_hbm, sib_hbm, *refs):
    pieces, (out_hbm, o_ref, n1_ref, own_ref, sib_ref, out_ref, sem) = refs[:-7], refs[-7:]
    items = 4
    y, zb, group, core = place()
    zb = zb if turn else 0
    width = own_hbm.shape[2]
    half = width // 2
    part = half // 2
    first = [
        pltpu.make_async_copy(own_hbm, own_ref, sem.at[items]),
        pltpu.make_async_copy(sib_hbm, sib_ref, sem.at[items + 1]),
    ]
    for copy in first:
        copy.start()
    for m in range(items):
        plan = plans[m // 2] if plans else None
        steps = steps_of(plan, roots_ref, y, group if m < 2 else 1 - group)
        step = steps[m % 2]
        column = y if m % 2 == 0 else 1 - y
        for ref, (item, far, halves) in zip(pieces, layout):
            if item != m:
                continue
            side = 1 - core if far else core
            for h, offset in halves:
                source = ref if len(halves) == 1 else ref.at[h]
                count = source.shape[1]
                for s in range(2):
                    row = jnp.where(column == 1, side, s) * half + offset
                    row = row + (1 - zb if h else zb) * part
                    col = jnp.where(column == 1, s, side) * half
                    pltpu.make_async_copy(
                        source.at[:, :, s * half : (s + 1) * half],
                        o_ref.at[
                            step,
                            :,
                            pl.ds(pl.multiple_of(row, count), count),
                            pl.ds(pl.multiple_of(col, half), half),
                        ],
                        sem.at[step],
                    ).start()

    def arrived(step):
        pltpu.make_async_copy(o_ref.at[step], o_ref.at[step], sem.at[step]).wait()

    for copy in first:
        copy.wait()
    arrived(0)
    for f, ref in ((core, own_ref), (1 - core, sib_ref)):
        at = pl.ds(pl.multiple_of(f * half, half), half)
        t = complex_dot(ref[0], ref[1], o_ref[0, 0], o_ref[0, 1])
        for p in range(2):
            value = t[p].astype(BF16)
            for e in range(2):
                n1_ref[e, p, :, at] = value[:, e * half : (e + 1) * half]
    mine = pl.ds(pl.multiple_of(core * half, half), half)
    arrived(1)
    arrived(2)
    o12 = complex_dot(o_ref[1, 0], o_ref[1, 1], o_ref[2, 0, :, mine], o_ref[2, 1, :, mine])
    o12 = [v.astype(BF16) for v in o12]
    arrived(3)
    rows = own_ref.shape[1]
    copies = []
    for r in range(2):
        band = slice(r * rows // 2, (r + 1) * rows // 2)
        n4 = [complex_dot(n1_ref[e, 0, band], n1_ref[e, 1, band], *o12) for e in range(2)]
        n4 = [jnp.concatenate([n4[0][p], n4[1][p]], 1).astype(BF16) for p in range(2)]
        made = complex_dot(*n4, o_ref[3, 0], o_ref[3, 1])
        for p in range(2):
            out_ref[p, band] = made[p]
        copy = pltpu.make_async_copy(
            out_ref.at[:, band], out_hbm.at[:, band], sem.at[items + 2 + r]
        )
        copy.start()
        copies.append(copy)
    for copy in copies:
        copy.wait()


def stem_call(plans, turn, roots, own, sib, items):
    shape = own.shape
    width = shape[2]
    pieces, layout = [], []
    for m, item in enumerate(items):
        for array, far, halves in item:
            pieces.append(array)
            layout.append((m, far, halves))
    anywhere = pl.BlockSpec(memory_space=pl.ANY)
    return pl.pallas_call(
        functools.partial(stem_kernel, plans, turn, tuple(layout)),
        grid_spec=pltpu.PrefetchScalarGridSpec(
            num_scalar_prefetch=1,
            grid=(1,),
            in_specs=[anywhere] * (2 + len(pieces)),
            out_specs=anywhere,
            scratch_shapes=[
                pltpu.VMEM((len(items), 2, width, width), BF16),
                pltpu.VMEM((2, *shape), BF16),
                pltpu.VMEM(shape, BF16),
                pltpu.VMEM(shape, BF16),
                pltpu.VMEM(shape, F32),
                pltpu.SemaphoreType.DMA((len(items) + 4,)),
            ],
        ),
        out_shape=jax.ShapeDtypeStruct(shape, F32),
        compiler_params=pltpu.CompilerParams(vmem_limit_bytes=LIMIT),
    )(roots, own, sib, *pieces)


def swap(value, axis, bit):
    n = lax.axis_size(axis)
    return lax.ppermute(value, axis, [(i, i ^ bit) for i in range(n)])


def other_core(value):
    return swap(value, "narrow", 1)


def select_kernel(plan, roots_ref, made_ref, other_ref, out_ref):
    y, _, group, _ = place()
    step, _ = steps_of(plan, roots_ref, y, group)
    owned = roots_ref[step] >> 2 == group

    @pl.when(owned)
    def _():
        out_ref[...] = made_ref[...]

    @pl.when(jnp.logical_not(owned))
    def _():
        out_ref[...] = other_ref[...]


def select_call(plan, roots, made, other):
    return pl.pallas_call(
        functools.partial(select_kernel, plan),
        grid_spec=pltpu.PrefetchScalarGridSpec(
            num_scalar_prefetch=1,
            grid=(1,),
            in_specs=[whole(made.shape)] * 2,
            out_specs=whole(made.shape),
        ),
        out_shape=jax.ShapeDtypeStruct(made.shape, made.dtype),
        compiler_params=pltpu.CompilerParams(vmem_limit_bytes=LIMIT),
    )(roots, made, other)


def after(value, other):
    return lax.optimization_barrier((value, other))[0]


def sends_of(leaves, roots, modes, plan, chunks):
    rows = leaves.shape[-1] // lax.axis_size("narrow")
    return leaf_call(send_kernel, SEND_LIMIT, chunks, rows // chunks, plan, roots, modes, leaves)


def tree(leaves, roots, modes, plan, sends, joint, cuts, ahead=None, sent=None):
    width = leaves.shape[-1]
    rows = width // lax.axis_size("narrow")
    chunks = len(sends)
    if sent is not None:
        leaves = after(leaves, sent)
    [keep] = leaf_call(keep_kernel, KEEP_LIMIT, 1, width, plan, roots, modes, leaves)
    lefts = [swap(send, "wide", 1) for send in sends]
    pairs = [
        call(pair_kernel, [left, keep], [jax.ShapeDtypeStruct(left.shape, BF16)])[0]
        for left in lefts
    ]
    gots = [swap(pair, "wide", 2) for pair in pairs]
    held = gots if ahead is None else [after(got, ahead) for got in gots]
    sibs = [other_core(v) for v in pairs + held]
    piece = jax.ShapeDtypeStruct((2, rows // 2, width), BF16)
    cut = jax.ShapeDtypeStruct((2, rows // 2 // cuts, width), BF16)
    other = jax.ShapeDtypeStruct((2, *piece.shape), BF16) if joint else piece
    made = call(
        functools.partial(branch_kernel, chunks, cuts), pairs + gots + sibs, [cut] * cuts + [other]
    )
    return made[:-1], made[-1]


def item_of(firsts, seconds):
    item = []
    for half, group in enumerate((firsts, seconds)):
        for i, piece in enumerate(group):
            place_of = ((half, i * piece.shape[1]),)
            item += [(piece, False, place_of), (other_core(piece), True, place_of)]
    return item


def joint_item(both):
    place_of = ((0, 0), (1, 0))
    return [(both, False, place_of), (other_core(both), True, place_of)]


def all_swapped(values, bit):
    return [swap(value, "wide", bit) for value in values]


def each_own_two(stem, leaves, roots, modes):
    own = stem.astype(BF16)
    sib = other_core(own)
    firsts, both = tree(
        leaves, roots, modes, None, sends_of(leaves, roots, modes, None, CHUNKS_TWO), True, CUTS_TWO
    )
    far = all_swapped(firsts, 4)
    near = [joint_item(both), joint_item(swap(both, "wide", 1))]
    far_second = all_swapped(far, 2)
    away = [item_of(far, far_second), item_of(all_swapped(far, 1), all_swapped(far, 3))]
    return stem_call(None, True, roots, own, sib, near + away)


def any_owners(stem, leaves, roots, modes):
    y, zb, group, _ = place()
    own = stem.astype(BF16)
    sib = other_core(own)
    two = lax.axis_size("wide") == 8
    items, plans, ahead = [], [], None
    every = [(k, k + 1) for k in range(0, leaves.shape[1], 2)]
    sends = [sends_of(leaves, roots, modes, plan, CHUNKS_FOUR) for plan in every]
    for j, plan in enumerate(every):
        firsts, second = tree(
            leaves,
            roots,
            modes,
            plan,
            sends[j],
            False,
            CUTS_FOUR if two else 1,
            ahead,
            sends[1][0] if j == 0 else None,
        )
        owned = roots[2 * j + y] // 4 == group
        if two:
            crossed = all_swapped(firsts, 4)
            ahead = crossed[0]
            here = [select_call(plan, roots, v, c) for v, c in zip(firsts, crossed)]
            seconds = all_swapped(here, 2)
            cross = [all_swapped(here, 1), all_swapped(here, 3)]
        else:
            sums = [
                lax.psum(
                    jnp.where(owned & (zb == 0) & (y == side), v, jnp.zeros_like(v)), "wide"
                )
                for side in range(2)
                for v in (firsts[0], second)
            ]
            here, seconds = ([jnp.where(y == 0, a, b)] for a, b in zip(sums[:2], sums[2:]))
            cross = [[jnp.where(y == 0, b, a)] for a, b in zip(sums[:2], sums[2:])]
        items += [item_of(here, seconds), item_of(*cross)]
        plans.append(plan)
    return stem_call(tuple(plans), two, roots, own, sib, items)


MODE = "cond"


def local(stem_tensor, leaves, root_devices, mode_orders):
    given = (stem_tensor, leaves, root_devices, mode_orders)
    if lax.axis_size("wide") != 8 or MODE == "four":
        return any_owners(*given)
    if MODE == "two":
        return each_own_two(*given)
    return lax.cond(jnp.sum(root_devices // 4) == 2, each_own_two, any_owners, *given)


def solution(mesh):
    placed = (
        P(None, ("cuts", "wide", "narrow"), None),
        P(("cuts", "wide"), None, None, None, None),
        P(),
        P(),
    )
    return jax.shard_map(
        local,
        mesh=mesh,
        in_specs=placed,
        out_specs=P(None, ("cuts", "wide", "narrow"), None),
        check_vma=False,
    )
```

```python
import functools

import jax
import jax.numpy as jnp
from jax import lax
from jax.experimental import pallas as pl
from jax.experimental.pallas import tpu as pltpu
from jax.sharding import PartitionSpec as P

F32, BF16, I32 = jnp.float32, jnp.bfloat16, jnp.int32
NN = (((1,), (0,)), ((), ()))
NT = (((1,), (1,)), ((), ()))
LIMIT = 48 * 1024 * 1024
SEND_LIMIT = 61 * 1024 * 1024
KEEP_LIMIT = 48 * 1024 * 1024
CHUNKS_TWO, CHUNKS_FOUR = 2, 2
CUTS_TWO, CUTS_FOUR = 1, 1


def dot(left, right, dims=NN):
    return lax.dot_general(left, right, dims, preferred_element_type=F32)


def complex_dot(lr, li, rr, ri):
    left = jnp.concatenate([lr, li], 1)
    return (
        dot(left, jnp.concatenate([rr, -ri], 0)),
        dot(left, jnp.concatenate([ri, rr], 0)),
    )


def source_of(column, modes_ref, step, modes, permuted):
    total = jnp.zeros_like(column)
    for b in range(modes):
        weight = jnp.left_shift(jnp.int32(1), modes_ref[step, b])
        total = total + jnp.where((column >> b) & 1 == 1, weight, 0)
    return jnp.where(permuted == 1, total, column)


def place():
    w = lax.axis_index("wide")
    return w & 1, w >> 1 & 1, w >> 2, lax.axis_index("narrow")


def steps_of(plan, roots_ref, y, group):
    if plan is not None:
        low, high = (jnp.int32(k) for k in plan)
    else:
        low = high = None
        for k in range(roots_ref.shape[0]):
            mine = roots_ref[k] >> 2 == group
            high = jnp.where(mine, k, 0 if high is None else high)
        for k in reversed(range(roots_ref.shape[0])):
            mine = roots_ref[k] >> 2 == group
            low = jnp.where(mine, k, k if low is None else low)
    return jnp.where(y == 0, low, high), jnp.where(y == 0, high, low)


def send_kernel(plan, roots_ref, modes_ref, leaves_ref, *refs):
    sends, (leaf_ref, sem) = refs[:-2], refs[-2:]
    part, width = sends[0].shape[1:]
    rows = part * len(sends)
    y, zb, group, core = place()
    _, step = steps_of(plan, roots_ref, y, group)

    @pl.when(y == 0)
    def _():
        copies = []
        for i, send_ref in enumerate(sends):
            at = pl.ds(pl.multiple_of(core * rows + i * part, part), part)
            copies.append(
                pltpu.make_async_copy(leaves_ref.at[0, step, :, at], send_ref, sem.at[i])
            )
            copies[-1].start()
        for copy in copies:
            copy.wait()

    @pl.when(y == 1)
    def _():
        copy = pltpu.make_async_copy(leaves_ref.at[0, step], leaf_ref, sem.at[0])
        copy.start()
        column = lax.broadcasted_iota(I32, (rows, 1), 0) + core * rows
        source = source_of(column, modes_ref, step, modes_ref.shape[1], zb)
        picked = lax.broadcasted_iota(I32, (rows, width), 1) == source
        picked = jnp.where(picked, 1.0, 0.0).astype(BF16)
        copy.wait()
        for p in range(2):
            made = dot(picked, leaf_ref[p], NT).astype(BF16)
            for i, send_ref in enumerate(sends):
                send_ref[p] = made[i * part : (i + 1) * part]


def keep_kernel(plan, roots_ref, modes_ref, leaves_ref, keep_ref, leaf_ref, sem):
    width = keep_ref.shape[2]
    y, zb, group, core = place()
    step, _ = steps_of(plan, roots_ref, y, group)
    copy = pltpu.make_async_copy(leaves_ref.at[0, step], leaf_ref, sem.at[0])
    copy.start()
    copy.wait()

    @pl.when(y == 0)
    def _():
        same = lax.broadcasted_iota(I32, (width, width), 0) == lax.broadcasted_iota(
            I32, (width, width), 1
        )
        same = jnp.where(same, 1.0, 0.0).astype(BF16)
        for p in range(2):
            keep_ref[p] = dot(same, leaf_ref[p], NT).astype(BF16)

    @pl.when(y == 1)
    def _():
        column = lax.broadcasted_iota(I32, (1, width), 1)
        source = source_of(column, modes_ref, step, modes_ref.shape[1], zb)
        picked = lax.broadcasted_iota(I32, (width, width), 0) == source
        picked = jnp.where(picked, 1.0, 0.0).astype(BF16)
        for p in range(2):
            keep_ref[p] = dot(leaf_ref[p], picked).astype(BF16)


def leaf_call(kernel, limit, parts, rows, plan, roots, modes, leaves):
    width = leaves.shape[-1]
    return pl.pallas_call(
        functools.partial(kernel, plan),
        grid_spec=pltpu.PrefetchScalarGridSpec(
            num_scalar_prefetch=2,
            grid=(1,),
            in_specs=[pl.BlockSpec(memory_space=pl.ANY)],
            out_specs=[whole((2, rows, width))] * parts,
            scratch_shapes=[pltpu.VMEM((2, width, width), BF16), pltpu.SemaphoreType.DMA((parts,))],
        ),
        out_shape=[jax.ShapeDtypeStruct((2, rows, width), BF16)] * parts,
        compiler_params=pltpu.CompilerParams(vmem_limit_bytes=limit),
    )(roots, modes, leaves)


def whole(shape):
    return pl.BlockSpec(shape, lambda i, *_: (0,) * len(shape))


def call(kernel, arrays, outs):
    return pl.pallas_call(
        kernel,
        grid=(1,),
        in_specs=[whole(a.shape) for a in arrays],
        out_specs=[whole(o.shape) for o in outs],
        out_shape=outs,
        compiler_params=pltpu.CompilerParams(vmem_limit_bytes=LIMIT),
    )(*arrays)


def pair_kernel(left_ref, right_ref, out_ref):
    re, im = complex_dot(left_ref[0], left_ref[1], right_ref[0], right_ref[1])
    out_ref[0] = re.astype(BF16)
    out_ref[1] = im.astype(BF16)


def branch_kernel(chunks, cuts, *refs):
    own, got, own_sib, got_sib = (refs[i * chunks : (i + 1) * chunks] for i in range(4))
    firsts, other_ref = refs[4 * chunks : 4 * chunks + cuts], refs[4 * chunks + cuts]
    y, zb, _, core = place()
    rows, width = own[0].shape[1] * chunks, own[0].shape[2]
    part = rows // 2
    high_here = y == zb

    def joined(group, p, at=slice(None)):
        values = [ref[p, :, at] for ref in group]
        return values[0] if len(values) == 1 else jnp.concatenate(values, 0)

    def multiply(left, near, far):
        re = im = None
        for side, right in ((core, near), (1 - core, far)):
            at = pl.ds(pl.multiple_of(side * rows, rows), rows)
            r, m = complex_dot(
                joined(left, 0, at), joined(left, 1, at), joined(right, 0), joined(right, 1)
            )
            re, im = (r, m) if re is None else (re + r, im + m)
        return re.astype(BF16), im.astype(BF16)

    def store(p, top, bottom):
        for here, first, second in ((0, top, bottom), (1, bottom, top)):

            @pl.when(zb == here)
            def _():
                for i, ref in enumerate(firsts):
                    ref[p] = first[i * part // cuts : (i + 1) * part // cuts]
                if len(other_ref.shape) == 4:
                    other_ref[0, p] = first
                    other_ref[1, p] = second
                else:
                    other_ref[p] = second

    def finish(parts):
        @pl.when(y == 1)
        def _():
            for p, value in enumerate(parts):
                store(p, value[:part], value[part:])

        @pl.when(y == 0)
        def _():
            same = lax.broadcasted_iota(I32, (rows, rows), 0) == lax.broadcasted_iota(
                I32, (rows, rows), 1
            )
            same = jnp.where(same, 1.0, 0.0).astype(BF16)
            for p, value in enumerate(parts):
                turned = [dot(same, value[:, i : i + rows], NT) for i in range(0, width, rows)]
                both = jnp.concatenate(turned, 1).astype(BF16)
                store(p, both[:part], both[part:])

    @pl.when(high_here)
    def _():
        finish(multiply(got, own, own_sib))

    @pl.when(jnp.logical_not(high_here))
    def _():
        finish(multiply(own, got, got_sib))


def stem_kernel(plans, turn, layout, roots_ref, own_hbm, sib_hbm, *refs):
    pieces, (out_hbm, o_ref, n1_ref, own_ref, sib_ref, out_ref, sem) = refs[:-7], refs[-7:]
    items = 4
    y, zb, group, core = place()
    zb = zb if turn else 0
    width = own_hbm.shape[2]
    half = width // 2
    part = half // 2
    first = [
        pltpu.make_async_copy(own_hbm, own_ref, sem.at[items]),
        pltpu.make_async_copy(sib_hbm, sib_ref, sem.at[items + 1]),
    ]
    for copy in first:
        copy.start()
    for m in range(items):
        plan = plans[m // 2] if plans else None
        steps = steps_of(plan, roots_ref, y, group if m < 2 else 1 - group)
        step = steps[m % 2]
        column = y if m % 2 == 0 else 1 - y
        for ref, (item, far, halves) in zip(pieces, layout):
            if item != m:
                continue
            side = 1 - core if far else core
            for h, offset in halves:
                source = ref if len(halves) == 1 else ref.at[h]
                count = source.shape[1]
                at = offset + (1 - zb if h else zb) * part

                @pl.when(column == 1)
                def _():
                    row = pl.ds(pl.multiple_of(side * half + at, count), count)
                    pltpu.make_async_copy(
                        source, o_ref.at[step, :, row], sem.at[step]
                    ).start()

                @pl.when(column == 0)
                def _():
                    col = pl.ds(pl.multiple_of(side * half, half), half)
                    for s in range(2):
                        row = pl.ds(pl.multiple_of(s * half + at, count), count)
                        pltpu.make_async_copy(
                            source.at[:, :, s * half : (s + 1) * half],
                            o_ref.at[step, :, row, col],
                            sem.at[step],
                        ).start()

    def arrived(step):
        pltpu.make_async_copy(o_ref.at[step], o_ref.at[step], sem.at[step]).wait()

    for copy in first:
        copy.wait()
    arrived(0)
    for f, ref in ((core, own_ref), (1 - core, sib_ref)):
        at = pl.ds(pl.multiple_of(f * half, half), half)
        t = complex_dot(ref[0], ref[1], o_ref[0, 0], o_ref[0, 1])
        for p in range(2):
            value = t[p].astype(BF16)
            for e in range(2):
                n1_ref[e, p, :, at] = value[:, e * half : (e + 1) * half]
    mine = pl.ds(pl.multiple_of(core * half, half), half)
    arrived(1)
    arrived(2)
    o12 = complex_dot(o_ref[1, 0], o_ref[1, 1], o_ref[2, 0, :, mine], o_ref[2, 1, :, mine])
    o12 = [v.astype(BF16) for v in o12]
    arrived(3)
    rows = own_ref.shape[1]
    copies = []
    for r in range(2):
        band = slice(r * rows // 2, (r + 1) * rows // 2)
        n4 = [complex_dot(n1_ref[e, 0, band], n1_ref[e, 1, band], *o12) for e in range(2)]
        n4 = [jnp.concatenate([n4[0][p], n4[1][p]], 1).astype(BF16) for p in range(2)]
        made = complex_dot(*n4, o_ref[3, 0], o_ref[3, 1])
        for p in range(2):
            out_ref[p, band] = made[p]
        copy = pltpu.make_async_copy(
            out_ref.at[:, band], out_hbm.at[:, band], sem.at[items + 2 + r]
        )
        copy.start()
        copies.append(copy)
    for copy in copies:
        copy.wait()


def stem_call(plans, turn, roots, own, sib, items):
    shape = own.shape
    width = shape[2]
    pieces, layout = [], []
    for m, item in enumerate(items):
        for array, far, halves in item:
            pieces.append(array)
            layout.append((m, far, halves))
    anywhere = pl.BlockSpec(memory_space=pl.ANY)
    return pl.pallas_call(
        functools.partial(stem_kernel, plans, turn, tuple(layout)),
        grid_spec=pltpu.PrefetchScalarGridSpec(
            num_scalar_prefetch=1,
            grid=(1,),
            in_specs=[anywhere] * (2 + len(pieces)),
            out_specs=anywhere,
            scratch_shapes=[
                pltpu.VMEM((len(items), 2, width, width), BF16),
                pltpu.VMEM((2, *shape), BF16),
                pltpu.VMEM(shape, BF16),
                pltpu.VMEM(shape, BF16),
                pltpu.VMEM(shape, F32),
                pltpu.SemaphoreType.DMA((len(items) + 4,)),
            ],
        ),
        out_shape=jax.ShapeDtypeStruct(shape, F32),
        compiler_params=pltpu.CompilerParams(vmem_limit_bytes=LIMIT),
    )(roots, own, sib, *pieces)


def swap(value, axis, bit):
    n = lax.axis_size(axis)
    return lax.ppermute(value, axis, [(i, i ^ bit) for i in range(n)])


def other_core(value):
    return swap(value, "narrow", 1)


def select_kernel(plan, roots_ref, made_ref, other_ref, out_ref):
    y, _, group, _ = place()
    step, _ = steps_of(plan, roots_ref, y, group)
    owned = roots_ref[step] >> 2 == group

    @pl.when(owned)
    def _():
        out_ref[...] = made_ref[...]

    @pl.when(jnp.logical_not(owned))
    def _():
        out_ref[...] = other_ref[...]


def select_call(plan, roots, made, other):
    return pl.pallas_call(
        functools.partial(select_kernel, plan),
        grid_spec=pltpu.PrefetchScalarGridSpec(
            num_scalar_prefetch=1,
            grid=(1,),
            in_specs=[whole(made.shape)] * 2,
            out_specs=whole(made.shape),
        ),
        out_shape=jax.ShapeDtypeStruct(made.shape, made.dtype),
        compiler_params=pltpu.CompilerParams(vmem_limit_bytes=LIMIT),
    )(roots, made, other)


def after(value, other):
    return lax.optimization_barrier((value, other))[0]


def sends_of(leaves, roots, modes, plan, chunks):
    rows = leaves.shape[-1] // lax.axis_size("narrow")
    return leaf_call(send_kernel, SEND_LIMIT, chunks, rows // chunks, plan, roots, modes, leaves)


def tree(leaves, roots, modes, plan, sends, joint, cuts, ahead=None, sent=None):
    width = leaves.shape[-1]
    rows = width // lax.axis_size("narrow")
    chunks = len(sends)
    if sent is not None:
        leaves = after(leaves, sent)
    [keep] = leaf_call(keep_kernel, KEEP_LIMIT, 1, width, plan, roots, modes, leaves)
    lefts = [swap(send, "wide", 1) for send in sends]
    pairs = [
        call(pair_kernel, [left, keep], [jax.ShapeDtypeStruct(left.shape, BF16)])[0]
        for left in lefts
    ]
    gots = [swap(pair, "wide", 2) for pair in pairs]
    held = gots if ahead is None else [after(got, ahead) for got in gots]
    sibs = [other_core(v) for v in pairs + held]
    piece = jax.ShapeDtypeStruct((2, rows // 2, width), BF16)
    cut = jax.ShapeDtypeStruct((2, rows // 2 // cuts, width), BF16)
    other = jax.ShapeDtypeStruct((2, *piece.shape), BF16) if joint else piece
    made = call(
        functools.partial(branch_kernel, chunks, cuts), pairs + gots + sibs, [cut] * cuts + [other]
    )
    return made[:-1], made[-1]


def item_of(firsts, seconds):
    item = []
    for half, group in enumerate((firsts, seconds)):
        for i, piece in enumerate(group):
            place_of = ((half, i * piece.shape[1]),)
            item += [(piece, False, place_of), (other_core(piece), True, place_of)]
    return item


def joint_item(both):
    place_of = ((0, 0), (1, 0))
    return [(both, False, place_of), (other_core(both), True, place_of)]


def all_swapped(values, bit):
    return [swap(value, "wide", bit) for value in values]


def each_own_two(stem, leaves, roots, modes):
    own = stem.astype(BF16)
    sib = other_core(own)
    firsts, both = tree(
        leaves, roots, modes, None, sends_of(leaves, roots, modes, None, CHUNKS_TWO), True, CUTS_TWO
    )
    far = all_swapped(firsts, 4)
    near = [joint_item(both), joint_item(swap(both, "wide", 1))]
    far_second = all_swapped(far, 2)
    away = [item_of(far, far_second), item_of(all_swapped(far, 1), all_swapped(far, 3))]
    return stem_call(None, True, roots, own, sib, near + away)


def any_owners(stem, leaves, roots, modes):
    y, zb, group, _ = place()
    own = stem.astype(BF16)
    sib = other_core(own)
    two = lax.axis_size("wide") == 8
    items, plans, ahead = [], [], None
    every = [(k, k + 1) for k in range(0, leaves.shape[1], 2)]
    sends = [sends_of(leaves, roots, modes, plan, CHUNKS_FOUR) for plan in every]
    for j, plan in enumerate(every):
        firsts, second = tree(
            leaves,
            roots,
            modes,
            plan,
            sends[j],
            False,
            CUTS_FOUR if two else 1,
            ahead,
            sends[1][0] if j == 0 else None,
        )
        owned = roots[2 * j + y] // 4 == group
        if two:
            crossed = all_swapped(firsts, 4)
            ahead = crossed[0]
            here = [select_call(plan, roots, v, c) for v, c in zip(firsts, crossed)]
            seconds = all_swapped(here, 2)
            cross = [all_swapped(here, 1), all_swapped(here, 3)]
        else:
            sums = [
                lax.psum(
                    jnp.where(owned & (zb == 0) & (y == side), v, jnp.zeros_like(v)), "wide"
                )
                for side in range(2)
                for v in (firsts[0], second)
            ]
            here, seconds = ([jnp.where(y == 0, a, b)] for a, b in zip(sums[:2], sums[2:]))
            cross = [[jnp.where(y == 0, b, a)] for a, b in zip(sums[:2], sums[2:])]
        items += [item_of(here, seconds), item_of(*cross)]
        plans.append(plan)
    return stem_call(tuple(plans), two, roots, own, sib, items)


MODE = "cond"


def local(stem_tensor, leaves, root_devices, mode_orders):
    given = (stem_tensor, leaves, root_devices, mode_orders)
    if lax.axis_size("wide") != 8 or MODE == "four":
        return any_owners(*given)
    if MODE == "two":
        return each_own_two(*given)
    return lax.cond(jnp.sum(root_devices // 4) == 2, each_own_two, any_owners, *given)


def solution(mesh):
    placed = (
        P(None, ("cuts", "wide", "narrow"), None),
        P(("cuts", "wide"), None, None, None, None),
        P(),
        P(),
    )
    return jax.shard_map(
        local,
        mesh=mesh,
        in_specs=placed,
        out_specs=P(None, ("cuts", "wide", "narrow"), None),
        check_vma=False,
    )
```
